768 devices in a mesh: fsdp: 64 (over z_hi, y, core), dp: 12 (over z_lo, x).
Axes of the slice: x: 4, y: 8, z: 12 (z_hi: 4, z_lo: 3; z = z_hi * 3 + z_lo), core: 2. Of those that a mesh axis runs over, the one named last changes fastest.
Arguments:
- inputs: bfloat16 [147456, 4096], P(('fsdp', 'dp')), may hold values from -6 to 6
- output_gradient_rows: bfloat16 [147456, 512], P(('fsdp', 'dp')), may hold values from -6 to 6
- fixed_value_weight: bfloat16 [4096, 512], P('fsdp'), may hold values from -0.09375 to 0.09375
- task_down_adapters: bfloat16 [12, 4096, 64], P('dp'), may hold values from -0.09375 to 0.09375
- task_up_adapters: bfloat16 [12, 64, 512], P('dp'), may hold values from -0.75 to 0.75
- live_row_counts: int32 [768, 12], P(('fsdp', 'dp')), may hold values from 0 to 16, as said below
- row_packing_order: int32 [768, 192], P(('fsdp', 'dp')), may hold values from 0 to 191, each once within a row
Outputs:
- input_grad: bfloat16 [147456, 4096], P(('fsdp', 'dp'))
- down_grad: float32 [12, 4096, 64], P('dp', 'fsdp')
- up_grad: float32 [12, 64, 512], P('dp', None, 'fsdp')
The draws below stay inside these ranges and needn't reach their ends.
Inputs may be any that keep to these rules, and one draw needn't show every extreme that they name: `live_row_counts`: for some task, every device of one fsdp index holds 16 live rows of it. Each row of row_packing_order is a permutation.
All inputs are finite; a program needn't handle non-finite values.
Results may differ from the reference program's by a relative error of at most 0.007.
Values may be sent and summed in bfloat16 or wider, within the bound.
No kernel may reach another device: no remote copies, remote signals or barrier semaphores. Data moves between devices by JAX's collectives and lax.ppermute only.
A program may use at most 64 MiB of HBM per device.

```python
import jax
import jax.numpy as jnp
from jax import lax

MODEL_FEATURES = 4096
VALUE_FEATURES = 512
ADAPTER_RANK = 64
SLOT = 16
TASK_COUNT = 12
ROWS_DEV = 192
ROWS = 147456
N_FSDP = 64
N_DP = 12


def draw_live_row_counts(key, part):
    key = jax.random.fold_in(key, 5)
    first, second, third, fourth = jax.random.split(key, 4)
    devices = N_FSDP * N_DP
    ceiling = jax.random.randint(first, (TASK_COUNT,), SLOT // 3, SLOT + 1)
    floors = ceiling // 2
    fraction = jax.random.randint(second, (devices, TASK_COUNT), 0, 1 << 20)
    counts = floors[None, :] + fraction * (ceiling - floors + 1)[None, :] // (1 << 20)
    chosen_column = jax.random.randint(third, (), 0, N_FSDP)
    chosen_task = jax.random.randint(fourth, (), 0, TASK_COUNT)
    device_index = jax.lax.broadcasted_iota(jnp.int32, (devices, TASK_COUNT), 0)
    task_index = jax.lax.broadcasted_iota(jnp.int32, (devices, TASK_COUNT), 1)
    forced = (device_index // N_DP == chosen_column) & (task_index == chosen_task)
    return jnp.where(forced, SLOT, counts).astype(jnp.int32)


def shard_levels(stream_key, extent, cuts, least, high):
    level, own = 1.0, jax.random.fold_in(stream_key, 6)
    for axis_at, blocks in cuts:
        steps = jnp.exp(jax.random.uniform(jax.random.fold_in(own, axis_at), (blocks,), jnp.float32, least / len(cuts), high / len(cuts)))
        level = level * jnp.repeat(steps, extent[axis_at] // blocks).reshape([-1 if axis == axis_at else 1 for axis in range(len(extent))])
    return level


def bell_draw(stream_key, shape, width, reach, pieces=(), kind=jnp.bfloat16):
    factor_of = shard_levels(stream_key, shape, pieces, -0.22, 0.18) if pieces else 1.0
    entries = jax.random.normal(stream_key, shape, jnp.float32) * width * factor_of
    return jnp.minimum(jnp.maximum(entries, -reach), reach).astype(kind)


def setup_inputs(seed: int = 0) -> dict:
    streams_of = jax.random.split(jax.random.key(seed), 8)
    return {
        "inputs": bell_draw(streams_of[0], (ROWS, MODEL_FEATURES), 1.0, 6.0, ((0, 768),)),
        "output_gradient_rows": bell_draw(streams_of[1], (ROWS, VALUE_FEATURES), 1.0, 6.0, ((0, 768),)),
        "fixed_value_weight": bell_draw(streams_of[2], (MODEL_FEATURES, VALUE_FEATURES), MODEL_FEATURES ** -0.5, 0.09375, ((0, 64),)),
        "task_down_adapters": bell_draw(streams_of[3], (TASK_COUNT, MODEL_FEATURES, ADAPTER_RANK), MODEL_FEATURES ** -0.5, 0.09375, ((0, 12),)),
        "task_up_adapters": bell_draw(streams_of[4], (TASK_COUNT, ADAPTER_RANK, VALUE_FEATURES), ADAPTER_RANK ** -0.5, 0.75, ((0, 12),)),
        "live_row_counts": draw_live_row_counts(jax.random.fold_in(streams_of[7], 71), 0),
        "row_packing_order": jax.vmap(lambda own: jax.random.permutation(own, ROWS_DEV))(jax.random.split(streams_of[6], (N_FSDP * N_DP))).reshape((N_FSDP * N_DP, ROWS_DEV)).astype(jnp.int32),
    }


ADAPTER_SCALING = 2.0


def reference(inputs, output_gradient_rows, fixed_value_weight, task_down_adapters, task_up_adapters, live_row_counts, row_packing_order):
    devices = row_packing_order.shape[0]
    task_groupings = task_down_adapters.shape[0]
    per_device = row_packing_order.shape[1]
    slot_rows = per_device // task_groupings
    features = inputs.shape[1]
    kv_width = output_gradient_rows.shape[1]
    adapter_rank_width = task_down_adapters.shape[2]
    row_blocks = inputs.reshape(devices, per_device, features)
    grad_blocks = output_gradient_rows.reshape(devices, per_device, kv_width)
    down_adapter_wide = task_down_adapters.astype(jnp.float32)
    up_adapter_wide = task_up_adapters.astype(jnp.float32)
    position = (jnp.arange(per_device, dtype=jnp.int32) % slot_rows).reshape(task_groupings, slot_rows)

    def one_device(carry, device_item):
        down_gradient_total, up_gradient_total = carry
        device_rows, device_grads, packing, counts = device_item
        is_live = position < counts[:, None]
        packed_rows = device_rows[packing].reshape(task_groupings, slot_rows, features)
        packed_grads = device_grads[packing].reshape(task_groupings, slot_rows, kv_width)
        packed_grads = jnp.where(is_live[:, :, None], packed_grads, jnp.zeros((), packed_grads.dtype))
        frozen_dx = jnp.dot(device_grads, fixed_value_weight.T, preferred_element_type=jnp.float32).astype(jnp.bfloat16)
        wide_input_rows = packed_rows.astype(jnp.float32)
        wide_output_gradients = packed_grads.astype(jnp.float32)
        down_projected_rows = jnp.einsum("gsd,gdr->gsr", wide_input_rows, down_adapter_wide).astype(jnp.bfloat16)
        gradient_projected = jnp.einsum("gsk,grk->gsr", wide_output_gradients, up_adapter_wide).astype(jnp.bfloat16)
        adapter_input_gradient = (ADAPTER_SCALING * jnp.einsum("nxe,nfe->nxf", gradient_projected.astype(jnp.float32), down_adapter_wide)).astype(jnp.bfloat16)
        placed = jnp.zeros((per_device, features), jnp.bfloat16).at[packing].set(adapter_input_gradient.reshape(per_device, features))
        device_dx = (frozen_dx.astype(jnp.float32) + placed.astype(jnp.float32)).astype(jnp.bfloat16)
        down_gradient_total = down_gradient_total + ADAPTER_SCALING * jnp.einsum("bnc,bnp->bcp", wide_input_rows, gradient_projected.astype(jnp.float32))
        up_gradient_total = up_gradient_total + ADAPTER_SCALING * jnp.einsum("vwz,vwj->vzj", down_projected_rows.astype(jnp.float32), wide_output_gradients)
        return (down_gradient_total, up_gradient_total), device_dx

    initial = (jnp.zeros((task_groupings, features, adapter_rank_width), jnp.float32), jnp.zeros((task_groupings, adapter_rank_width, kv_width), jnp.float32))
    (down_grad, up_grad), input_grad = lax.scan(one_device, initial, (row_blocks, grad_blocks, row_packing_order, live_row_counts))
    return input_grad.reshape(devices * per_device, features), down_grad, up_grad
```

```python
import functools

import jax
import jax.numpy as jnp
import numpy as np
from jax import lax
from jax.experimental import pallas as pl
from jax.experimental.pallas import tpu as pltpu
from jax.sharding import Mesh, PartitionSpec as P

ADAPTER_SCALING = 2.0
FSDP = ("zh", "y", "c")
DP = ("zl", "x")
VMEM_LIMIT = 48 * 1024 * 1024
NT = (((1,), (1,)), ((), ()))
NN = (((1,), (0,)), ((), ()))
TN = (((0,), (0,)), ((), ()))


def dot(a, b, dims):
    return lax.dot_general(a, b, dims, preferred_element_type=jnp.float32)


def live_one_hot(counts_ref, packing_ref):
    per_device = packing_ref.shape[1]
    tasks = counts_ref.shape[1]
    slot = per_device // tasks
    lane = lax.broadcasted_iota(jnp.int32, (1, per_device), 1)
    key = jnp.full((1, per_device), -1, jnp.int32)
    packing = packing_ref[...]
    for t in range(tasks):
        mine = (lane >= t * slot) & (lane < t * slot + counts_ref[0, t])
        key = jnp.where(mine, packing, key)
    row = lax.broadcasted_iota(jnp.int32, (per_device, per_device), 0)
    return jnp.where(row == key, 1.0, 0.0).astype(jnp.bfloat16)


def pack_kernel(counts_ref, packing_ref, rows_ref, grads_ref, out_ref):
    chosen = live_one_hot(counts_ref, packing_ref)
    features = rows_ref.shape[1]
    step = 1024
    for at in range(0, features, step):
        out_ref[:, at : at + step] = dot(chosen, rows_ref[:, at : at + step], TN).astype(jnp.bfloat16)
    out_ref[:, features:] = dot(chosen, grads_ref[...], TN).astype(jnp.bfloat16)


def input_grad_kernel(grads_ref, down_t_ref, up_ref, dx_ref, proj_ref):
    proj = dot(grads_ref[...], up_ref[...], NT).astype(jnp.bfloat16)
    proj_ref[...] = proj
    features = down_t_ref.shape[1]
    step = 1024
    for at in range(0, features, step):
        dx = ADAPTER_SCALING * dot(proj, down_t_ref[:, at : at + step], NN)
        dx_ref[:, at : at + step] = dx.astype(jnp.bfloat16)


def weight_grad_kernel(core_ref, recv_ref, down_t_ref, proj_ref, keep_ref, send_ref):
    rank, features = down_t_ref.shape
    blocks = keep_ref.shape[0]
    first = core_ref[0] == 0
    wide = features // blocks
    half = wide // 2
    quarter = half // 2
    proj = proj_ref[...]
    total = jnp.zeros((recv_ref.shape[0], rank), jnp.float32)
    step = 1024
    for at in range(0, features, step):
        rows = recv_ref[:, at : at + step]
        total = total + dot(rows, down_t_ref[:, at : at + step], NT)
        down = ADAPTER_SCALING * dot(rows, proj, TN)
        for b in range(step // wide):
            pair = []
            for c in range(2):
                lo = b * wide + c * half
                pair.append(jnp.concatenate([down[lo : lo + quarter], down[lo + quarter : lo + half]], axis=1))
            keep_ref[at // wide + b, :quarter, :] = jnp.where(first, pair[0], pair[1])
            send_ref[at // wide + b, :quarter, :] = jnp.where(first, pair[1], pair[0])
    grads = recv_ref[:, features:]
    up_t = ADAPTER_SCALING * dot(grads, total.astype(jnp.bfloat16), TN)
    up_t = jnp.concatenate([up_t, jnp.zeros_like(up_t)], axis=1)
    few = grads.shape[1] // (2 * blocks)
    for b in range(blocks):
        low, high = up_t[2 * b * few : (2 * b + 1) * few], up_t[(2 * b + 1) * few : (2 * b + 2) * few]
        keep_ref[b, quarter:, :] = jnp.where(first, low, high)
        send_ref[b, quarter:, :] = jnp.where(first, high, low)


def final_kernel(core_ref, counts_ref, packing_ref, grads_ref, own_ref, other_ref, back_ref, out_ref, chosen_ref):
    @pl.when(pl.program_id(0) == 0)
    def _():
        chosen_ref[...] = live_one_hot(counts_ref, packing_ref)

    first = core_ref[0] == 0
    several, _, part, depth = own_ref.shape
    own, other = own_ref[:, 0], other_ref[:, 0]
    low = jnp.where(first, own, other)
    high = jnp.where(first, other, own)
    weight = jnp.concatenate([low, high], axis=1).reshape(several * 2 * part, depth)
    frozen = dot(grads_ref[...], weight, NT).astype(jnp.bfloat16)
    placed = dot(chosen_ref[...], back_ref[...], NN)
    out_ref[...] = (frozen.astype(jnp.float32) + placed).astype(jnp.bfloat16)


def whole():
    return pl.BlockSpec(memory_space=pltpu.VMEM)


def scalars():
    return pl.BlockSpec(memory_space=pltpu.SMEM)


def params():
    return pltpu.CompilerParams(vmem_limit_bytes=VMEM_LIMIT)


def on_device(
    inputs,
    output_gradient_rows,
    fixed_value_weight,
    task_down_adapters,
    task_up_adapters,
    live_row_counts,
    row_packing_order,
):
    per_device, features = inputs.shape
    kv_width = output_gradient_rows.shape[1]
    tasks = lax.axis_size("zl") * lax.axis_size("x")
    slot = per_device // tasks
    n_zh, n_y = lax.axis_size("zh"), lax.axis_size("y")
    blocks = n_zh * n_y
    part = fixed_value_weight.shape[0]
    down_t = task_down_adapters[0].T
    up = task_up_adapters[0]
    rank = up.shape[0]
    bf16, f32 = jnp.bfloat16, jnp.float32
    core = lax.axis_index("c").astype(jnp.int32).reshape(1)

    with jax.named_scope("pack"):
        packed = pl.pallas_call(
            pack_kernel,
            out_shape=jax.ShapeDtypeStruct((per_device, features + kv_width), bf16),
            in_specs=[scalars(), whole(), whole(), whole()],
            out_specs=whole(),
            compiler_params=params(),
        )(live_row_counts, row_packing_order, inputs, output_gradient_rows)
        recv = lax.all_to_all(packed.reshape(tasks, slot, features + kv_width), DP, 0, 0, tiled=True)
        recv = recv.reshape(per_device, features + kv_width)

    with jax.named_scope("frozen_gather"):
        along_z = lax.all_gather(fixed_value_weight, "zh", axis=0, tiled=True)
        own = lax.all_gather(along_z, "y", axis=0, tiled=True)

    with jax.named_scope("adapter_input_grad"):
        dx, proj = pl.pallas_call(
            input_grad_kernel,
            out_shape=(
                jax.ShapeDtypeStruct((per_device, features), bf16),
                jax.ShapeDtypeStruct((per_device, rank), bf16),
            ),
            grid=(1,),
            in_specs=[
                pl.BlockSpec((per_device, kv_width), lambda i: (0, features // kv_width)),
                pl.BlockSpec((rank, features), lambda i: (0, 0)),
                pl.BlockSpec((rank, kv_width), lambda i: (0, 0)),
            ],
            out_specs=(
                pl.BlockSpec((per_device, features), lambda i: (0, 0)),
                pl.BlockSpec((per_device, rank), lambda i: (0, 0)),
            ),
            compiler_params=params(),
        )(recv, down_t, up)
        back = lax.all_to_all(dx.reshape(tasks, slot, features), DP, 0, 0, tiled=True)
        back = back.reshape(per_device, features)

    with jax.named_scope("weight_grads"):
        quarter = features // (4 * blocks)
        few = kv_width // (2 * blocks)
        terms = jax.ShapeDtypeStruct((blocks, quarter + few, 2 * rank), f32)
        keep, send = pl.pallas_call(
            weight_grad_kernel,
            out_shape=(terms, terms),
            in_specs=[scalars(), whole(), whole(), whole()],
            out_specs=(whole(), whole()),
            compiler_params=params(),
        )(core, recv, down_t, proj)
        chip = (keep + lax.ppermute(send, "c", [(0, 1), (1, 0)])).astype(bf16)
        chip, own = lax.optimization_barrier((chip, own))
        other = lax.ppermute(own, "c", [(0, 1), (1, 0)])
        chip, back = lax.optimization_barrier((chip, back))
        shares = lax.all_to_all(chip, ("zh", "y"), 0, 0, tiled=True)
        share = jnp.sum(shares.astype(f32), axis=0)
        down_share = jnp.concatenate([share[:quarter, :rank], share[:quarter, rank:]], axis=0)
        up_share = share[quarter:, :rank].T

    with jax.named_scope("input_grad"):
        halves = 2
        several = n_y // halves
        wide = several * 2 * part
        order = (n_y, n_zh, part, kv_width)
        weight_spec = pl.BlockSpec((several, 1, part, kv_width), lambda i: (i % halves, i // halves, 0, 0))
        input_grad = pl.pallas_call(
            final_kernel,
            out_shape=jax.ShapeDtypeStruct((per_device, features), bf16),
            grid=(features // wide,),
            in_specs=[
                scalars(),
                scalars(),
                pl.BlockSpec((1, per_device), lambda i: (0, 0)),
                pl.BlockSpec((per_device, kv_width), lambda i: (0, 0)),
                weight_spec,
                weight_spec,
                pl.BlockSpec((per_device, wide), lambda i: (0, i)),
            ],
            out_specs=pl.BlockSpec((per_device, wide), lambda i: (0, i)),
            scratch_shapes=[pltpu.VMEM((per_device, per_device), bf16)],
            compiler_params=params(),
        )(
            core,
            live_row_counts,
            row_packing_order,
            output_gradient_rows,
            own.reshape(order),
            other.reshape(order),
            back,
        )
    return (input_grad, down_share[None], up_share[None])


def solution(mesh, parts=(4, 8, 2, 3, 4)):
    fine = Mesh(np.asarray(mesh.devices).reshape(parts), FSDP + DP)
    rows = P(FSDP + DP, None)
    in_specs = (
        rows,
        rows,
        P(FSDP, None),
        P(DP, None, None),
        P(DP, None, None),
        rows,
        rows,
    )
    out_specs = (rows, P(DP, FSDP, None), P(DP, None, FSDP))
    return jax.shard_map(on_device, mesh=fine, in_specs=in_specs, out_specs=out_specs, check_vma=False)
```

```python
import functools

import jax
import jax.numpy as jnp
import numpy as np
from jax import lax
from jax.experimental import pallas as pl
from jax.experimental.pallas import tpu as pltpu
from jax.sharding import Mesh, PartitionSpec as P

ADAPTER_SCALING = 2.0
FSDP = ("zh", "y", "c")
DP = ("zl", "x")
VMEM_LIMIT = 16 * 1024 * 1024
WHOLE_VMEM = 60 * 1024 * 1024
NT = (((1,), (1,)), ((), ()))
NN = (((1,), (0,)), ((), ()))
TN = (((0,), (0,)), ((), ()))


def dot(a, b, dims):
    return lax.dot_general(a, b, dims, preferred_element_type=jnp.float32)


def live_one_hot(counts_ref, packing_ref):
    per_device = packing_ref.shape[1]
    tasks = counts_ref.shape[1]
    slot = per_device // tasks
    lane = lax.broadcasted_iota(jnp.int32, (1, per_device), 1)
    key = jnp.full((1, per_device), -1, jnp.int32)
    packing = packing_ref[...]
    for t in range(tasks):
        mine = (lane >= t * slot) & (lane < t * slot + counts_ref[0, t])
        key = jnp.where(mine, packing, key)
    row = lax.broadcasted_iota(jnp.int32, (per_device, per_device), 0)
    return jnp.where(row == key, 1.0, 0.0).astype(jnp.bfloat16)


def pack_kernel(counts_hbm, packing_hbm, rows_hbm, grads_hbm, out_hbm, counts, packing, held, packed, few_sems, in_sems, out_sems):
    features = rows_hbm.shape[1]
    width = grads_hbm.shape[1]
    pieces = in_sems.shape[0]
    step = features // (pieces - 1)
    spans = [pl.ds(at * step, step) for at in range(pieces - 1)] + [pl.ds(features, width)]
    small = (
        pltpu.make_async_copy(counts_hbm, counts, few_sems.at[0]),
        pltpu.make_async_copy(packing_hbm, packing, few_sems.at[1]),
    )
    loads = []
    for at, span in enumerate(spans):
        source = grads_hbm if at == pieces - 1 else rows_hbm.at[:, span]
        loads.append(pltpu.make_async_copy(source, held.at[:, span], in_sems.at[at]))
    for copy in (*small, *loads):
        copy.start()
    for copy in small:
        copy.wait()
    chosen = live_one_hot(counts, packing)
    stores = []
    for at, span in enumerate(spans):
        loads[at].wait()
        packed[:, span] = dot(chosen, held[:, span], TN).astype(jnp.bfloat16)
        stores.append(pltpu.make_async_copy(packed.at[:, span], out_hbm.at[:, span], out_sems.at[at]))
        stores[at].start()
    for copy in stores:
        copy.wait()


def input_grad_kernel(grads_ref, down_t_ref, up_ref, dx_ref):
    proj = dot(grads_ref[...], up_ref[...], NT).astype(jnp.bfloat16)
    features = down_t_ref.shape[1]
    step = 1024
    for at in range(0, features, step):
        dx = ADAPTER_SCALING * dot(proj, down_t_ref[:, at : at + step], NN)
        dx_ref[:, at : at + step] = dx.astype(jnp.bfloat16)


def weight_grad_kernel(core_ref, recv_ref, down_t_ref, up_ref, keep_ref, send_ref):
    rank, features = down_t_ref.shape
    blocks = keep_ref.shape[0]
    first = core_ref[0] == 0
    wide = features // blocks
    half = wide // 2
    quarter = half // 2
    grads = recv_ref[:, features:]
    proj = dot(grads, up_ref[...], NT).astype(jnp.bfloat16)
    total = jnp.zeros((recv_ref.shape[0], rank), jnp.float32)
    step = 1024
    for at in range(0, features, step):
        rows = recv_ref[:, at : at + step]
        total = total + dot(rows, down_t_ref[:, at : at + step], NT)
        down = ADAPTER_SCALING * dot(rows, proj, TN)
        for b in range(step // wide):
            pair = []
            for c in range(2):
                lo = b * wide + c * half
                pair.append(jnp.concatenate([down[lo : lo + quarter], down[lo + quarter : lo + half]], axis=1))
            keep_ref[at // wide + b, :quarter, :] = jnp.where(first, pair[0], pair[1])
            send_ref[at // wide + b, :quarter, :] = jnp.where(first, pair[1], pair[0])
    up_t = ADAPTER_SCALING * dot(grads, total.astype(jnp.bfloat16), TN)
    up_t = jnp.concatenate([up_t, jnp.zeros_like(up_t)], axis=1)
    few = grads.shape[1] // (2 * blocks)
    for b in range(blocks):
        low, high = up_t[2 * b * few : (2 * b + 1) * few], up_t[(2 * b + 1) * few : (2 * b + 2) * few]
        keep_ref[b, quarter:, :] = jnp.where(first, low, high)
        send_ref[b, quarter:, :] = jnp.where(first, high, low)


def final_kernel(place_ref, counts_ref, packing_ref, grads_ref, own_ref, other_ref, back_ref, out_ref, chosen_ref):
    @pl.when(pl.program_id(0) == 0)
    def _():
        chosen_ref[...] = live_one_hot(counts_ref, packing_ref)

    first = place_ref[0] == 0
    several, _, part, depth = own_ref.shape
    own, other = own_ref[:, 0], other_ref[:, 0]
    low = jnp.where(first, own, other)
    high = jnp.where(first, other, own)
    weight = jnp.concatenate([low, high], axis=1).reshape(several * 2 * part, depth)
    frozen = dot(grads_ref[...], weight, NT).astype(jnp.bfloat16)
    placed = dot(chosen_ref[...], back_ref[...], NN)
    out_ref[...] = (frozen.astype(jnp.float32) + placed).astype(jnp.bfloat16)


def one(*shape):
    return pl.BlockSpec(shape, lambda i: (0,) * len(shape))


def hbm():
    return pl.BlockSpec(memory_space=pltpu.HBM)


def scalars():
    return pl.BlockSpec(memory_space=pltpu.SMEM)


def params(limit=VMEM_LIMIT):
    return pltpu.CompilerParams(vmem_limit_bytes=limit)


def on_device(
    inputs,
    output_gradient_rows,
    fixed_value_weight,
    task_down_adapters,
    task_up_adapters,
    live_row_counts,
    row_packing_order,
):
    per_device, features = inputs.shape
    kv_width = output_gradient_rows.shape[1]
    tasks = lax.axis_size("zl") * lax.axis_size("x")
    slot = per_device // tasks
    n_zh, n_y = lax.axis_size("zh"), lax.axis_size("y")
    blocks = n_zh * n_y
    part = fixed_value_weight.shape[0]
    down_t = task_down_adapters[0].T
    up = task_up_adapters[0]
    rank = up.shape[0]
    bf16, f32 = jnp.bfloat16, jnp.float32
    core = lax.axis_index("c").astype(jnp.int32).reshape(1)

    with jax.named_scope("frozen_gather"):
        along_z = [fixed_value_weight]
        for shift in range(1, n_zh):
            along_z.append(lax.ppermute(fixed_value_weight, "zh", [(i, (i + shift) % n_zh) for i in range(n_zh)]))

    with jax.named_scope("pack"):
        packed = pl.pallas_call(
            pack_kernel,
            out_shape=jax.ShapeDtypeStruct((per_device, features + kv_width), bf16),
            in_specs=[hbm(), hbm(), hbm(), hbm()],
            out_specs=hbm(),
            scratch_shapes=[
                pltpu.SMEM((1, tasks), jnp.int32),
                pltpu.VMEM((1, per_device), jnp.int32),
                pltpu.VMEM((per_device, features + kv_width), bf16),
                pltpu.VMEM((per_device, features + kv_width), bf16),
                pltpu.SemaphoreType.DMA((2,)),
                pltpu.SemaphoreType.DMA((5,)),
                pltpu.SemaphoreType.DMA((5,)),
            ],
            compiler_params=params(WHOLE_VMEM),
        )(live_row_counts, row_packing_order, inputs, output_gradient_rows)
        packed, *along_z = lax.optimization_barrier((packed, *along_z))
        recv = lax.all_to_all(packed.reshape(tasks, slot, features + kv_width), DP, 0, 0, tiled=True)
        recv = recv.reshape(per_device, features + kv_width)
        own = lax.all_gather(jnp.concatenate(along_z, axis=0), "y", axis=0, tiled=True)

    with jax.named_scope("adapter_input_grad"):
        dx = pl.pallas_call(
            input_grad_kernel,
            out_shape=jax.ShapeDtypeStruct((per_device, features), bf16),
            grid=(1,),
            in_specs=[
                pl.BlockSpec((per_device, kv_width), lambda i: (0, features // kv_width)),
                one(rank, features),
                one(rank, kv_width),
            ],
            out_specs=one(per_device, features),
            compiler_params=params(),
        )(recv, down_t, up)
        back = lax.all_to_all(dx.reshape(tasks, slot, features), DP, 0, 0, tiled=True)
        back = back.reshape(per_device, features)

    with jax.named_scope("weight_grads"):
        quarter = features // (4 * blocks)
        few = kv_width // (2 * blocks)
        terms = jax.ShapeDtypeStruct((blocks, quarter + few, 2 * rank), f32)
        keep, send = pl.pallas_call(
            weight_grad_kernel,
            out_shape=(terms, terms),
            grid=(1,),
            in_specs=[scalars(), one(per_device, features + kv_width), one(rank, features), one(rank, kv_width)],
            out_specs=(one(*terms.shape), one(*terms.shape)),
            compiler_params=params(),
        )(core, recv, down_t, up)
        chip = (keep + lax.ppermute(send, "c", [(0, 1), (1, 0)])).astype(bf16)
        chip, own = lax.optimization_barrier((chip, own))
        other = lax.ppermute(own, "c", [(0, 1), (1, 0)])
        chip, back = lax.optimization_barrier((chip, back))
        shares = lax.all_to_all(chip, ("zh", "y"), 0, 0, tiled=True)
        share = jnp.sum(shares.astype(f32), axis=0)
        down_share = jnp.concatenate([share[:quarter, :rank], share[:quarter, rank:]], axis=0)
        up_share = share[quarter:, :rank].T

    with jax.named_scope("input_grad"):
        halves = 2
        several = n_y // halves
        wide = several * 2 * part
        order = (n_y, n_zh, part, kv_width)

        def block(*shape):
            return pl.BlockSpec(shape, lambda i, place: (0,) * len(shape))

        def weight_at(i, place):
            return i % halves, lax.rem(place[1] - i // halves + n_zh, n_zh), 0, 0

        weight_spec = pl.BlockSpec((several, 1, part, kv_width), weight_at)
        rows_spec = pl.BlockSpec((per_device, wide), lambda i, place: (0, i))
        place = jnp.stack([core[0], lax.axis_index("zh").astype(jnp.int32)])
        input_grad = pl.pallas_call(
            final_kernel,
            out_shape=jax.ShapeDtypeStruct((per_device, features), bf16),
            grid_spec=pltpu.PrefetchScalarGridSpec(
                num_scalar_prefetch=1,
                grid=(features // wide,),
                in_specs=[
                    scalars(),
                    block(1, per_device),
                    block(per_device, kv_width),
                    weight_spec,
                    weight_spec,
                    rows_spec,
                ],
                out_specs=rows_spec,
                scratch_shapes=[pltpu.VMEM((per_device, per_device), bf16)],
            ),
            compiler_params=params(),
        )(
            place,
            live_row_counts,
            row_packing_order,
            output_gradient_rows,
            own.reshape(order),
            other.reshape(order),
            back,
        )
    return (input_grad, down_share[None], up_share[None])


def solution(mesh, parts=(4, 8, 2, 3, 4)):
    fine = Mesh(np.asarray(mesh.devices).reshape(parts), FSDP + DP)
    rows = P(FSDP + DP, None)
    in_specs = (
        rows,
        rows,
        P(FSDP, None),
        P(DP, None, None),
        P(DP, None, None),
        rows,
        rows,
    )
    out_specs = (rows, P(DP, FSDP, None), P(DP, None, FSDP))
    return jax.shard_map(on_device, mesh=fine, in_specs=in_specs, out_specs=out_specs, check_vma=False)
```

```python
import functools

import jax
import jax.numpy as jnp
import numpy as np
from jax import lax
from jax.experimental import pallas as pl
from jax.experimental.pallas import tpu as pltpu
from jax.sharding import Mesh, PartitionSpec as P

ADAPTER_SCALING = 2.0
FSDP = ("zh", "y", "c")
DP = ("zl", "x")
VMEM_LIMIT = 16 * 1024 * 1024
WHOLE_VMEM = 60 * 1024 * 1024
NT = (((1,), (1,)), ((), ()))
NN = (((1,), (0,)), ((), ()))
TN = (((0,), (0,)), ((), ()))


def dot(a, b, dims):
    return lax.dot_general(a, b, dims, preferred_element_type=jnp.float32)


def live_one_hot(counts_ref, packing_ref):
    per_device = packing_ref.shape[1]
    tasks = counts_ref.shape[1]
    slot = per_device // tasks
    lane = lax.broadcasted_iota(jnp.int32, (1, per_device), 1)
    key = jnp.full((1, per_device), -1, jnp.int32)
    packing = packing_ref[...]
    for t in range(tasks):
        mine = (lane >= t * slot) & (lane < t * slot + counts_ref[0, t])
        key = jnp.where(mine, packing, key)
    row = lax.broadcasted_iota(jnp.int32, (per_device, per_device), 0)
    return jnp.where(row == key, 1.0, 0.0).astype(jnp.bfloat16)


def pack_kernel(counts_hbm, packing_hbm, rows_hbm, grads_hbm, out_hbm, counts, packing, held, packed, few_sems, in_sems, out_sems):
    features = rows_hbm.shape[1]
    width = grads_hbm.shape[1]
    pieces = in_sems.shape[0]
    step = features // (pieces - 1)
    spans = [pl.ds(at * step, step) for at in range(pieces - 1)] + [pl.ds(features, width)]
    small = (
        pltpu.make_async_copy(counts_hbm, counts, few_sems.at[0]),
        pltpu.make_async_copy(packing_hbm, packing, few_sems.at[1]),
    )
    loads = []
    for at, span in enumerate(spans):
        source = grads_hbm if at == pieces - 1 else rows_hbm.at[:, span]
        loads.append(pltpu.make_async_copy(source, held.at[:, span], in_sems.at[at]))
    for copy in (*small, *loads):
        copy.start()
    for copy in small:
        copy.wait()
    chosen = live_one_hot(counts, packing)
    stores = []
    for at, span in enumerate(spans):
        loads[at].wait()
        packed[:, span] = dot(chosen, held[:, span], TN).astype(jnp.bfloat16)
        stores.append(pltpu.make_async_copy(packed.at[:, span], out_hbm.at[:, span], out_sems.at[at]))
        stores[at].start()
    for copy in stores:
        copy.wait()


def adapter_kernel(place_ref, recv_ref, down_t_ref, up_ref, dx_ref, keep_ref, send_ref):
    rank, features = down_t_ref.shape
    n_y, n_zh = keep_ref.shape[:2]
    blocks = n_y * n_zh
    first = place_ref[0] == 0
    wide = features // blocks
    half = wide // 2
    quarter = half // 2
    grads = recv_ref[:, features:]
    proj = dot(grads, up_ref[...], NT).astype(jnp.bfloat16)
    total = jnp.zeros((recv_ref.shape[0], rank), jnp.float32)
    step = 1024
    turn = [lax.rem(y - place_ref[1] + n_y, n_y) for y in range(n_y)]
    for at in range(0, features, step):
        rows = recv_ref[:, at : at + step]
        part = down_t_ref[:, at : at + step]
        dx_ref[:, at : at + step] = (ADAPTER_SCALING * dot(proj, part, NN)).astype(jnp.bfloat16)
        total = total + dot(rows, part, NT)
        down = ADAPTER_SCALING * dot(rows, proj, TN)
        for b in range(step // wide):
            zh, y = divmod(at // wide + b, n_y)
            pair = []
            for c in range(2):
                lo = b * wide + c * half
                pair.append(jnp.concatenate([down[lo : lo + quarter], down[lo + quarter : lo + half]], axis=1))
            keep_ref[turn[y], zh, :quarter, :] = jnp.where(first, pair[0], pair[1])
            send_ref[turn[y], zh, :quarter, :] = jnp.where(first, pair[1], pair[0])
    up_t = ADAPTER_SCALING * dot(grads, total.astype(jnp.bfloat16), TN)
    up_t = jnp.concatenate([up_t, jnp.zeros_like(up_t)], axis=1)
    few = grads.shape[1] // (2 * blocks)
    for b in range(blocks):
        zh, y = divmod(b, n_y)
        low, high = up_t[2 * b * few : (2 * b + 1) * few], up_t[(2 * b + 1) * few : (2 * b + 2) * few]
        keep_ref[turn[y], zh, quarter:, :] = jnp.where(first, low, high)
        send_ref[turn[y], zh, quarter:, :] = jnp.where(first, high, low)


def chip_sum_kernel(keep_ref, other_ref, own_ref, *away_refs):
    own_ref[...] = keep_ref[0] + other_ref[0]
    for at, away_ref in enumerate(away_refs):
        away_ref[...] = (keep_ref[at + 1] + other_ref[at + 1]).astype(away_ref.dtype)


def column_sum_kernel(own_ref, *refs):
    *got_refs, out_ref = refs
    total = own_ref[...]
    for got_ref in got_refs:
        total = total + got_ref[...].astype(jnp.float32)
    out_ref[...] = total


def last_sum_kernel(got_ref, down_ref, up_t_ref):
    half, rank = down_ref.shape
    quarter = half // 2
    total = jnp.sum(got_ref[...], axis=0)
    down_ref[:quarter, :] = total[:quarter, :rank]
    down_ref[quarter:, :] = total[:quarter, rank:]
    up_t_ref[...] = total[quarter:, :rank]


def final_kernel(place_ref, counts_ref, packing_ref, grads_ref, own_ref, other_ref, back_ref, out_ref, chosen_ref):
    @pl.when(pl.program_id(0) == 0)
    def _():
        chosen_ref[...] = live_one_hot(counts_ref, packing_ref)

    first = place_ref[0] == 0
    several, _, part, depth = own_ref.shape
    own, other = own_ref[:, 0], other_ref[:, 0]
    low = jnp.where(first, own, other)
    high = jnp.where(first, other, own)
    weight = jnp.concatenate([low, high], axis=1).reshape(several * 2 * part, depth)
    frozen = dot(grads_ref[...], weight, NT).astype(jnp.bfloat16)
    placed = dot(chosen_ref[...], back_ref[...], NN)
    out_ref[...] = (frozen.astype(jnp.float32) + placed).astype(jnp.bfloat16)


def one(*shape):
    return pl.BlockSpec(shape, lambda i: (0,) * len(shape))


def hbm():
    return pl.BlockSpec(memory_space=pltpu.HBM)


def scalars():
    return pl.BlockSpec(memory_space=pltpu.SMEM)


def params(limit=VMEM_LIMIT):
    return pltpu.CompilerParams(vmem_limit_bytes=limit)


def on_device(
    inputs,
    output_gradient_rows,
    fixed_value_weight,
    task_down_adapters,
    task_up_adapters,
    live_row_counts,
    row_packing_order,
):
    per_device, features = inputs.shape
    kv_width = output_gradient_rows.shape[1]
    tasks = lax.axis_size("zl") * lax.axis_size("x")
    slot = per_device // tasks
    n_zh, n_y = lax.axis_size("zh"), lax.axis_size("y")
    blocks = n_zh * n_y
    part = fixed_value_weight.shape[0]
    down_t = task_down_adapters[0].T
    up = task_up_adapters[0]
    rank = up.shape[0]
    bf16, f32 = jnp.bfloat16, jnp.float32
    place = jnp.stack([lax.axis_index("c"), lax.axis_index("y")]).astype(jnp.int32)

    with jax.named_scope("frozen_gather"):
        spread = jnp.broadcast_to(fixed_value_weight[None], (n_zh, part, kv_width))
        along_z = lax.all_to_all(spread, "zh", 0, 0, tiled=True).reshape(n_zh * part, kv_width)

    with jax.named_scope("pack"):
        packed = pl.pallas_call(
            pack_kernel,
            out_shape=jax.ShapeDtypeStruct((per_device, features + kv_width), bf16),
            in_specs=[hbm(), hbm(), hbm(), hbm()],
            out_specs=hbm(),
            scratch_shapes=[
                pltpu.SMEM((1, tasks), jnp.int32),
                pltpu.VMEM((1, per_device), jnp.int32),
                pltpu.VMEM((per_device, features + kv_width), bf16),
                pltpu.VMEM((per_device, features + kv_width), bf16),
                pltpu.SemaphoreType.DMA((2,)),
                pltpu.SemaphoreType.DMA((5,)),
                pltpu.SemaphoreType.DMA((5,)),
            ],
            compiler_params=params(WHOLE_VMEM),
        )(live_row_counts, row_packing_order, inputs, output_gradient_rows)
        packed, along_z = lax.optimization_barrier((packed, along_z))
        recv = lax.all_to_all(packed.reshape(tasks, slot, features + kv_width), DP, 0, 0, tiled=True)
        recv = recv.reshape(per_device, features + kv_width)
        own = lax.all_gather(along_z, "y", axis=0, tiled=True)

    with jax.named_scope("adapters"):
        quarter = features // (4 * blocks)
        few = kv_width // (2 * blocks)
        deep = quarter + few
        terms = jax.ShapeDtypeStruct((n_y, n_zh, deep, 2 * rank), f32)
        dx, keep, send = pl.pallas_call(
            adapter_kernel,
            out_shape=(jax.ShapeDtypeStruct((per_device, features), bf16), terms, terms),
            grid=(1,),
            in_specs=[scalars(), one(per_device, features + kv_width), one(rank, features), one(rank, kv_width)],
            out_specs=(one(per_device, features), one(*terms.shape), one(*terms.shape)),
            compiler_params=params(),
        )(place, recv, down_t, up)
        back = lax.all_to_all(dx.reshape(tasks, slot, features), DP, 0, 0, tiled=True)
        back = back.reshape(per_device, features)

    with jax.named_scope("weight_grads"):
        terms = (n_y, n_zh * deep, 2 * rank)
        flat = terms[1:]
        keep, from_core = keep.reshape(terms), lax.ppermute(send.reshape(terms), "c", [(0, 1), (1, 0)])
        mine, *away = pl.pallas_call(
            chip_sum_kernel,
            out_shape=[jax.ShapeDtypeStruct(flat, f32)] + [jax.ShapeDtypeStruct(flat, bf16)] * (n_y - 1),
            grid=(1,),
            in_specs=[one(*terms), one(*terms)],
            out_specs=[one(*flat)] * n_y,
            compiler_params=params(),
        )(keep, from_core)
        own, mine, *away = lax.optimization_barrier((own, mine, *away))
        other = lax.ppermute(own, "c", [(0, 1), (1, 0)])
        got = [lax.ppermute(a, "y", [(i, (i + at + 1) % n_y) for i in range(n_y)]) for at, a in enumerate(away)]
        column = pl.pallas_call(
            column_sum_kernel,
            out_shape=jax.ShapeDtypeStruct(flat, f32),
            grid=(1,),
            in_specs=[one(*flat)] * n_y,
            out_specs=one(*flat),
            compiler_params=params(),
        )(mine, *got)
        column, back = lax.optimization_barrier((column, back))
        shares = lax.all_to_all(column.reshape(n_zh, deep, 2 * rank), "zh", 0, 0, tiled=True)
        down_share, up_t_share = pl.pallas_call(
            last_sum_kernel,
            out_shape=(jax.ShapeDtypeStruct((2 * quarter, rank), f32), jax.ShapeDtypeStruct((few, rank), f32)),
            grid=(1,),
            in_specs=[one(n_zh, deep, 2 * rank)],
            out_specs=(one(2 * quarter, rank), one(few, rank)),
            compiler_params=params(),
        )(shares)
        up_share = up_t_share.T

    with jax.named_scope("input_grad"):
        halves = 1
        several = n_y // halves
        wide = several * 2 * part
        order = (n_y, n_zh, part, kv_width)

        def block(*shape):
            return pl.BlockSpec(shape, lambda i, place: (0,) * len(shape))

        weight_spec = pl.BlockSpec((several, 1, part, kv_width), lambda i, place: (i % halves, i // halves, 0, 0))
        rows_spec = pl.BlockSpec((per_device, wide), lambda i, place: (0, i))
        input_grad = pl.pallas_call(
            final_kernel,
            out_shape=jax.ShapeDtypeStruct((per_device, features), bf16),
            grid_spec=pltpu.PrefetchScalarGridSpec(
                num_scalar_prefetch=1,
                grid=(features // wide,),
                in_specs=[
                    scalars(),
                    block(1, per_device),
                    block(per_device, kv_width),
                    weight_spec,
                    weight_spec,
                    rows_spec,
                ],
                out_specs=rows_spec,
                scratch_shapes=[pltpu.VMEM((per_device, per_device), bf16)],
            ),
            compiler_params=params(WHOLE_VMEM),
        )(
            place,
            live_row_counts,
            row_packing_order,
            output_gradient_rows,
            own.reshape(order),
            other.reshape(order),
            back,
        )
    return (input_grad, down_share[None], up_share[None])


def solution(mesh, parts=(4, 8, 2, 3, 4)):
    fine = Mesh(np.asarray(mesh.devices).reshape(parts), FSDP + DP)
    rows = P(FSDP + DP, None)
    in_specs = (
        rows,
        rows,
        P(FSDP, None),
        P(DP, None, None),
        P(DP, None, None),
        rows,
        rows,
    )
    out_specs = (rows, P(DP, FSDP, None), P(DP, None, FSDP))
    return jax.shard_map(on_device, mesh=fine, in_specs=in_specs, out_specs=out_specs, check_vma=False)
```

```python
import functools

import jax
import jax.numpy as jnp
import numpy as np
from jax import lax
from jax.experimental import pallas as pl
from jax.experimental.pallas import tpu as pltpu
from jax.sharding import Mesh, PartitionSpec as P

ADAPTER_SCALING = 2.0
FSDP = ("zh", "y", "c")
DP = ("zl", "x")
VMEM_LIMIT = 16 * 1024 * 1024
WHOLE_VMEM = 60 * 1024 * 1024
NT = (((1,), (1,)), ((), ()))
NN = (((1,), (0,)), ((), ()))
TN = (((0,), (0,)), ((), ()))


def dot(a, b, dims):
    return lax.dot_general(a, b, dims, preferred_element_type=jnp.float32)


def live_one_hot(counts_ref, packing_ref):
    per_device = packing_ref.shape[1]
    tasks = counts_ref.shape[1]
    slot = per_device // tasks
    lane = lax.broadcasted_iota(jnp.int32, (1, per_device), 1)
    key = jnp.full((1, per_device), -1, jnp.int32)
    packing = packing_ref[...]
    for t in range(tasks):
        mine = (lane >= t * slot) & (lane < t * slot + counts_ref[0, t])
        key = jnp.where(mine, packing, key)
    row = lax.broadcasted_iota(jnp.int32, (per_device, per_device), 0)
    return jnp.where(row == key, 1.0, 0.0).astype(jnp.bfloat16)


def pack_kernel(counts_hbm, packing_hbm, rows_hbm, grads_hbm, out_hbm, counts, packing, held, packed, few_sems, in_sems, out_sems):
    features = rows_hbm.shape[1]
    width = grads_hbm.shape[1]
    pieces = in_sems.shape[0]
    step = features // (pieces - 1)
    spans = [pl.ds(at * step, step) for at in range(pieces - 1)] + [pl.ds(features, width)]
    small = (
        pltpu.make_async_copy(counts_hbm, counts, few_sems.at[0]),
        pltpu.make_async_copy(packing_hbm, packing, few_sems.at[1]),
    )
    loads = []
    for at, span in enumerate(spans):
        source = grads_hbm if at == pieces - 1 else rows_hbm.at[:, span]
        loads.append(pltpu.make_async_copy(source, held.at[:, span], in_sems.at[at]))
    for copy in (*small, *loads):
        copy.start()
    for copy in small:
        copy.wait()
    chosen = live_one_hot(counts, packing)
    stores = []
    for at, span in enumerate(spans):
        loads[at].wait()
        packed[:, span] = dot(chosen, held[:, span], TN).astype(jnp.bfloat16)
        stores.append(pltpu.make_async_copy(packed.at[:, span], out_hbm.at[:, span], out_sems.at[at]))
        stores[at].start()
    for copy in stores:
        copy.wait()


def adapter_kernel(place_ref, recv_ref, down_t_ref, up_ref, dx_ref, keep_ref, send_ref):
    rank, features = down_t_ref.shape
    n_y, n_zh = keep_ref.shape[:2]
    blocks = n_y * n_zh
    first = place_ref[0] == 0
    wide = features // blocks
    half = wide // 2
    quarter = half // 2
    grads = recv_ref[:, features:]
    proj = dot(grads, up_ref[...], NT).astype(jnp.bfloat16)
    total = jnp.zeros((recv_ref.shape[0], rank), jnp.float32)
    step = 1024
    for at in range(0, features, step):
        rows = recv_ref[:, at : at + step]
        part = down_t_ref[:, at : at + step]
        dx_ref[:, at : at + step] = (ADAPTER_SCALING * dot(proj, part, NN)).astype(jnp.bfloat16)
        total = total + dot(rows, part, NT)
        down = ADAPTER_SCALING * dot(rows, proj, TN)
        for b in range(step // wide):
            zh, y = divmod(at // wide + b, n_y)
            pair = []
            for c in range(2):
                lo = b * wide + c * half
                pair.append(jnp.concatenate([down[lo : lo + quarter], down[lo + quarter : lo + half]], axis=1))
            keep_ref[y, zh, :quarter, :] = jnp.where(first, pair[0], pair[1])
            send_ref[y, zh, :quarter, :] = jnp.where(first, pair[1], pair[0])
    up_t = ADAPTER_SCALING * dot(grads, total.astype(jnp.bfloat16), TN)
    up_t = jnp.concatenate([up_t, jnp.zeros_like(up_t)], axis=1)
    few = grads.shape[1] // (2 * blocks)
    for b in range(blocks):
        zh, y = divmod(b, n_y)
        low, high = up_t[2 * b * few : (2 * b + 1) * few], up_t[(2 * b + 1) * few : (2 * b + 2) * few]
        keep_ref[y, zh, quarter:, :] = jnp.where(first, low, high)
        send_ref[y, zh, quarter:, :] = jnp.where(first, high, low)


def chip_sum_kernel(keep_ref, other_ref, out_ref):
    out_ref[...] = keep_ref[...] + other_ref[...]


def last_sum_kernel(got_ref, down_ref, up_t_ref):
    half, rank = down_ref.shape
    quarter = half // 2
    total = jnp.sum(got_ref[...], axis=0)
    down_ref[:quarter, :] = total[:quarter, :rank]
    down_ref[quarter:, :] = total[:quarter, rank:]
    up_t_ref[...] = total[quarter:, :rank]


def final_kernel(place_ref, counts_ref, packing_ref, grads_ref, own_ref, other_ref, back_ref, out_ref, chosen_ref):
    @pl.when(pl.program_id(0) == 0)
    def _():
        chosen_ref[...] = live_one_hot(counts_ref, packing_ref)

    first = place_ref[0] == 0
    several, _, part, depth = own_ref.shape
    own, other = own_ref[:, 0], other_ref[:, 0]
    low = jnp.where(first, own, other)
    high = jnp.where(first, other, own)
    weight = jnp.concatenate([low, high], axis=1).reshape(several * 2 * part, depth)
    frozen = dot(grads_ref[...], weight, NT).astype(jnp.bfloat16)
    placed = dot(chosen_ref[...], back_ref[...], NN)
    out_ref[...] = (frozen.astype(jnp.float32) + placed).astype(jnp.bfloat16)


def one(*shape):
    return pl.BlockSpec(shape, lambda i: (0,) * len(shape))


def hbm():
    return pl.BlockSpec(memory_space=pltpu.HBM)


def scalars():
    return pl.BlockSpec(memory_space=pltpu.SMEM)


def params(limit=VMEM_LIMIT):
    return pltpu.CompilerParams(vmem_limit_bytes=limit)


def on_device(
    inputs,
    output_gradient_rows,
    fixed_value_weight,
    task_down_adapters,
    task_up_adapters,
    live_row_counts,
    row_packing_order,
):
    per_device, features = inputs.shape
    kv_width = output_gradient_rows.shape[1]
    tasks = lax.axis_size("zl") * lax.axis_size("x")
    slot = per_device // tasks
    n_zh, n_y = lax.axis_size("zh"), lax.axis_size("y")
    blocks = n_zh * n_y
    part = fixed_value_weight.shape[0]
    down_t = task_down_adapters[0].T
    up = task_up_adapters[0]
    rank = up.shape[0]
    bf16, f32 = jnp.bfloat16, jnp.float32
    place = lax.axis_index("c").astype(jnp.int32).reshape(1)

    with jax.named_scope("frozen_gather"):
        spread = jnp.broadcast_to(fixed_value_weight[None], (n_zh, part, kv_width))
        along_z = lax.all_to_all(spread, "zh", 0, 0, tiled=True).reshape(n_zh * part, kv_width)

    with jax.named_scope("pack"):
        packed = pl.pallas_call(
            pack_kernel,
            out_shape=jax.ShapeDtypeStruct((per_device, features + kv_width), bf16),
            in_specs=[hbm(), hbm(), hbm(), hbm()],
            out_specs=hbm(),
            scratch_shapes=[
                pltpu.SMEM((1, tasks), jnp.int32),
                pltpu.VMEM((1, per_device), jnp.int32),
                pltpu.VMEM((per_device, features + kv_width), bf16),
                pltpu.VMEM((per_device, features + kv_width), bf16),
                pltpu.SemaphoreType.DMA((2,)),
                pltpu.SemaphoreType.DMA((5,)),
                pltpu.SemaphoreType.DMA((5,)),
            ],
            compiler_params=params(WHOLE_VMEM),
        )(live_row_counts, row_packing_order, inputs, output_gradient_rows)
        packed, along_z = lax.optimization_barrier((packed, along_z))
        recv = lax.all_to_all(packed.reshape(tasks, slot, features + kv_width), DP, 0, 0, tiled=True)
        recv = recv.reshape(per_device, features + kv_width)
        own = lax.all_gather(along_z, "y", axis=0, tiled=True)

    with jax.named_scope("adapters"):
        quarter = features // (4 * blocks)
        few = kv_width // (2 * blocks)
        deep = quarter + few
        terms = jax.ShapeDtypeStruct((n_y, n_zh, deep, 2 * rank), f32)
        dx, keep, send = pl.pallas_call(
            adapter_kernel,
            out_shape=(jax.ShapeDtypeStruct((per_device, features), bf16), terms, terms),
            grid=(1,),
            in_specs=[scalars(), one(per_device, features + kv_width), one(rank, features), one(rank, kv_width)],
            out_specs=(one(per_device, features), one(*terms.shape), one(*terms.shape)),
            compiler_params=params(),
        )(place, recv, down_t, up)
        back = lax.all_to_all(dx.reshape(tasks, slot, features), DP, 0, 0, tiled=True)
        back = back.reshape(per_device, features)

    with jax.named_scope("weight_grads"):
        terms = (blocks * deep, 2 * rank)
        keep, from_core = keep.reshape(terms), lax.ppermute(send.reshape(terms), "c", [(0, 1), (1, 0)])
        chip = pl.pallas_call(
            chip_sum_kernel,
            out_shape=jax.ShapeDtypeStruct(terms, f32),
            grid=(1,),
            in_specs=[one(*terms), one(*terms)],
            out_specs=one(*terms),
            compiler_params=params(),
        )(keep, from_core)
        chip, own = lax.optimization_barrier((chip, own))
        other = lax.ppermute(own, "c", [(0, 1), (1, 0)])
        column = lax.psum_scatter(chip, "y", scatter_dimension=0, tiled=True)
        column, back = lax.optimization_barrier((column, back))
        shares = lax.all_to_all(column.reshape(n_zh, deep, 2 * rank), "zh", 0, 0, tiled=True)
        down_share, up_t_share = pl.pallas_call(
            last_sum_kernel,
            out_shape=(jax.ShapeDtypeStruct((2 * quarter, rank), f32), jax.ShapeDtypeStruct((few, rank), f32)),
            grid=(1,),
            in_specs=[one(n_zh, deep, 2 * rank)],
            out_specs=(one(2 * quarter, rank), one(few, rank)),
            compiler_params=params(),
        )(shares)
        up_share = up_t_share.T

    with jax.named_scope("input_grad"):
        halves = 1
        several = n_y // halves
        wide = several * 2 * part
        order = (n_y, n_zh, part, kv_width)

        def block(*shape):
            return pl.BlockSpec(shape, lambda i, place: (0,) * len(shape))

        weight_spec = pl.BlockSpec((several, 1, part, kv_width), lambda i, place: (i % halves, i // halves, 0, 0))
        rows_spec = pl.BlockSpec((per_device, wide), lambda i, place: (0, i))
        input_grad = pl.pallas_call(
            final_kernel,
            out_shape=jax.ShapeDtypeStruct((per_device, features), bf16),
            grid_spec=pltpu.PrefetchScalarGridSpec(
                num_scalar_prefetch=1,
                grid=(features // wide,),
                in_specs=[
                    scalars(),
                    block(1, per_device),
                    block(per_device, kv_width),
                    weight_spec,
                    weight_spec,
                    rows_spec,
                ],
                out_specs=rows_spec,
                scratch_shapes=[pltpu.VMEM((per_device, per_device), bf16)],
            ),
            compiler_params=params(WHOLE_VMEM),
        )(
            place,
            live_row_counts,
            row_packing_order,
            output_gradient_rows,
            own.reshape(order),
            other.reshape(order),
            back,
        )
    return (input_grad, down_share[None], up_share[None])


def solution(mesh, parts=(4, 8, 2, 3, 4)):
    fine = Mesh(np.asarray(mesh.devices).reshape(parts), FSDP + DP)
    rows = P(FSDP + DP, None)
    in_specs = (
        rows,
        rows,
        P(FSDP, None),
        P(DP, None, None),
        P(DP, None, None),
        rows,
        rows,
    )
    out_specs = (rows, P(DP, FSDP, None), P(DP, None, FSDP))
    return jax.shard_map(on_device, mesh=fine, in_specs=in_specs, out_specs=out_specs, check_vma=False)
```

```python
import functools

import jax
import jax.numpy as jnp
import numpy as np
from jax import lax
from jax.experimental import pallas as pl
from jax.experimental.pallas import tpu as pltpu
from jax.sharding import Mesh, PartitionSpec as P

ADAPTER_SCALING = 2.0
FSDP = ("zh", "y", "c")
DP = ("zl", "x")
VMEM_LIMIT = 16 * 1024 * 1024
WHOLE_VMEM = 60 * 1024 * 1024
NT = (((1,), (1,)), ((), ()))
NN = (((1,), (0,)), ((), ()))
TN = (((0,), (0,)), ((), ()))


def dot(a, b, dims):
    return lax.dot_general(a, b, dims, preferred_element_type=jnp.float32)


def live_one_hot(counts_ref, packing_ref):
    per_device = packing_ref.shape[1]
    tasks = counts_ref.shape[1]
    slot = per_device // tasks
    lane = lax.broadcasted_iota(jnp.int32, (1, per_device), 1)
    key = jnp.full((1, per_device), -1, jnp.int32)
    packing = packing_ref[...]
    for t in range(tasks):
        mine = (lane >= t * slot) & (lane < t * slot + counts_ref[0, t])
        key = jnp.where(mine, packing, key)
    row = lax.broadcasted_iota(jnp.int32, (per_device, per_device), 0)
    return jnp.where(row == key, 1.0, 0.0).astype(jnp.bfloat16)


def pack_kernel(counts_hbm, packing_hbm, rows_hbm, grads_hbm, out_hbm, counts, packing, held, packed, few_sems, in_sems, out_sems):
    features = rows_hbm.shape[1]
    width = grads_hbm.shape[1]
    pieces = in_sems.shape[0]
    step = features // (pieces - 1)
    spans = [pl.ds(at * step, step) for at in range(pieces - 1)] + [pl.ds(features, width)]
    small = (
        pltpu.make_async_copy(counts_hbm, counts, few_sems.at[0]),
        pltpu.make_async_copy(packing_hbm, packing, few_sems.at[1]),
    )
    loads = []
    for at, span in enumerate(spans):
        source = grads_hbm if at == pieces - 1 else rows_hbm.at[:, span]
        loads.append(pltpu.make_async_copy(source, held.at[:, span], in_sems.at[at]))
    for copy in (*small, *loads):
        copy.start()
    for copy in small:
        copy.wait()
    chosen = live_one_hot(counts, packing)
    stores = []
    for at, span in enumerate(spans):
        loads[at].wait()
        packed[:, span] = dot(chosen, held[:, span], TN).astype(jnp.bfloat16)
        stores.append(pltpu.make_async_copy(packed.at[:, span], out_hbm.at[:, span], out_sems.at[at]))
        stores[at].start()
    for copy in stores:
        copy.wait()


def adapter_kernel(place_ref, recv_ref, down_t_ref, up_ref, dx_ref, keep_ref, send_ref):
    rank, features = down_t_ref.shape
    n_y, n_zh = keep_ref.shape[:2]
    blocks = n_y * n_zh
    first = place_ref[0] == 0
    wide = features // blocks
    half = wide // 2
    quarter = half // 2
    grads = recv_ref[:, features:]
    proj = dot(grads, up_ref[...], NT).astype(jnp.bfloat16)
    total = jnp.zeros((recv_ref.shape[0], rank), jnp.float32)
    step = 1024
    turn = []
    for y in range(n_y):
        apart, at, bit = lax.bitwise_xor(place_ref[1], y), 0, n_y // 2
        while bit:
            at = at + (apart % 2) * bit
            apart, bit = apart // 2, bit // 2
        turn.append(at)
    for at in range(0, features, step):
        rows = recv_ref[:, at : at + step]
        part = down_t_ref[:, at : at + step]
        dx_ref[:, at : at + step] = (ADAPTER_SCALING * dot(proj, part, NN)).astype(jnp.bfloat16)
        total = total + dot(rows, part, NT)
        down = ADAPTER_SCALING * dot(rows, proj, TN)
        for b in range(step // wide):
            zh, y = divmod(at // wide + b, n_y)
            pair = []
            for c in range(2):
                lo = b * wide + c * half
                pair.append(jnp.concatenate([down[lo : lo + quarter], down[lo + quarter : lo + half]], axis=1))
            keep_ref[turn[y], zh, :quarter, :] = jnp.where(first, pair[0], pair[1])
            send_ref[turn[y], zh, :quarter, :] = jnp.where(first, pair[1], pair[0])
    up_t = ADAPTER_SCALING * dot(grads, total.astype(jnp.bfloat16), TN)
    up_t = jnp.concatenate([up_t, jnp.zeros_like(up_t)], axis=1)
    few = grads.shape[1] // (2 * blocks)
    for b in range(blocks):
        zh, y = divmod(b, n_y)
        low, high = up_t[2 * b * few : (2 * b + 1) * few], up_t[(2 * b + 1) * few : (2 * b + 2) * few]
        keep_ref[turn[y], zh, quarter:, :] = jnp.where(first, low, high)
        send_ref[turn[y], zh, quarter:, :] = jnp.where(first, high, low)


def half_kernel(held_ref, got_ref, keep_ref, send_ref):
    half = keep_ref.shape[0]
    keep_ref[...] = held_ref[:half] + got_ref[:half].astype(jnp.float32)
    send_ref[...] = (held_ref[half:] + got_ref[half:].astype(jnp.float32)).astype(send_ref.dtype)


def add_kernel(held_ref, got_ref, out_ref):
    out_ref[...] = held_ref[...] + got_ref[...].astype(jnp.float32)


def last_sum_kernel(got_ref, down_ref, up_t_ref):
    half, rank = down_ref.shape
    quarter = half // 2
    total = jnp.sum(got_ref[...], axis=0)
    down_ref[:quarter, :] = total[:quarter, :rank]
    down_ref[quarter:, :] = total[:quarter, rank:]
    up_t_ref[...] = total[quarter:, :rank]


def final_kernel(place_ref, counts_ref, packing_ref, grads_ref, own_ref, other_ref, back_ref, out_ref, chosen_ref):
    @pl.when(pl.program_id(0) == 0)
    def _():
        chosen_ref[...] = live_one_hot(counts_ref, packing_ref)

    first = place_ref[0] == 0
    several, _, part, depth = own_ref.shape
    own, other = own_ref[:, 0], other_ref[:, 0]
    low = jnp.where(first, own, other)
    high = jnp.where(first, other, own)
    weight = jnp.concatenate([low, high], axis=1).reshape(several * 2 * part, depth)
    frozen = dot(grads_ref[...], weight, NT).astype(jnp.bfloat16)
    placed = dot(chosen_ref[...], back_ref[...], NN)
    out_ref[...] = (frozen.astype(jnp.float32) + placed).astype(jnp.bfloat16)


def one(*shape):
    return pl.BlockSpec(shape, lambda i: (0,) * len(shape))


def hbm():
    return pl.BlockSpec(memory_space=pltpu.HBM)


def scalars():
    return pl.BlockSpec(memory_space=pltpu.SMEM)


def params(limit=VMEM_LIMIT):
    return pltpu.CompilerParams(vmem_limit_bytes=limit)


def on_device(
    inputs,
    output_gradient_rows,
    fixed_value_weight,
    task_down_adapters,
    task_up_adapters,
    live_row_counts,
    row_packing_order,
):
    per_device, features = inputs.shape
    kv_width = output_gradient_rows.shape[1]
    tasks = lax.axis_size("zl") * lax.axis_size("x")
    slot = per_device // tasks
    n_zh, n_y = lax.axis_size("zh"), lax.axis_size("y")
    blocks = n_zh * n_y
    part = fixed_value_weight.shape[0]
    down_t = task_down_adapters[0].T
    up = task_up_adapters[0]
    rank = up.shape[0]
    bf16, f32 = jnp.bfloat16, jnp.float32
    place = jnp.stack([lax.axis_index("c"), lax.axis_index("y"), lax.axis_index("zh")]).astype(jnp.int32)

    with jax.named_scope("frozen_gather"):
        along_z = [fixed_value_weight]
        for shift in range(1, n_zh):
            along_z.append(lax.ppermute(fixed_value_weight, "zh", [(i, (i + shift) % n_zh) for i in range(n_zh)]))
        own = lax.all_gather(jnp.concatenate(along_z, axis=0), "y", axis=0, tiled=True)

    with jax.named_scope("pack"):
        packed = pl.pallas_call(
            pack_kernel,
            out_shape=jax.ShapeDtypeStruct((per_device, features + kv_width), bf16),
            in_specs=[hbm(), hbm(), hbm(), hbm()],
            out_specs=hbm(),
            scratch_shapes=[
                pltpu.SMEM((1, tasks), jnp.int32),
                pltpu.VMEM((1, per_device), jnp.int32),
                pltpu.VMEM((per_device, features + kv_width), bf16),
                pltpu.VMEM((per_device, features + kv_width), bf16),
                pltpu.SemaphoreType.DMA((2,)),
                pltpu.SemaphoreType.DMA((5,)),
                pltpu.SemaphoreType.DMA((5,)),
            ],
            compiler_params=params(WHOLE_VMEM),
        )(live_row_counts, row_packing_order, inputs, output_gradient_rows)
        recv = lax.all_to_all(packed.reshape(tasks, slot, features + kv_width), DP, 0, 0, tiled=True)
        recv = recv.reshape(per_device, features + kv_width)
        recv, *along_z = lax.optimization_barrier((recv, *along_z))

    with jax.named_scope("adapters"):
        quarter = features // (4 * blocks)
        few = kv_width // (2 * blocks)
        deep = quarter + few
        terms = jax.ShapeDtypeStruct((n_y, n_zh, deep, 2 * rank), f32)
        dx, keep, send = pl.pallas_call(
            adapter_kernel,
            out_shape=(jax.ShapeDtypeStruct((per_device, features), bf16), terms, terms),
            grid=(1,),
            in_specs=[scalars(), one(per_device, features + kv_width), one(rank, features), one(rank, kv_width)],
            out_specs=(one(per_device, features), one(*terms.shape), one(*terms.shape)),
            compiler_params=params(),
        )(place, recv, down_t, up)
        back = lax.all_to_all(dx.reshape(tasks, slot, features), DP, 0, 0, tiled=True)
        back = back.reshape(per_device, features)

    with jax.named_scope("weight_grads"):
        flat = (n_zh * deep, 2 * rank)
        held, got = keep.reshape(n_y, *flat), lax.ppermute(send.reshape(n_y, *flat), "c", [(0, 1), (1, 0)])
        count, apart = n_y, 1
        while count > 1:
            count //= 2
            held, away = pl.pallas_call(
                half_kernel,
                out_shape=(jax.ShapeDtypeStruct((count, *flat), f32), jax.ShapeDtypeStruct((count, *flat), bf16)),
                grid=(1,),
                in_specs=[one(2 * count, *flat), one(2 * count, *flat)],
                out_specs=(one(count, *flat), one(count, *flat)),
                compiler_params=params(),
            )(held, got)
            got = lax.ppermute(away, "y", [(i, i ^ apart) for i in range(n_y)])
            apart *= 2
        column = pl.pallas_call(
            add_kernel,
            out_shape=jax.ShapeDtypeStruct((1, *flat), f32),
            grid=(1,),
            in_specs=[one(1, *flat), one(1, *flat)],
            out_specs=one(1, *flat),
            compiler_params=params(),
        )(held, got)
        column, own = lax.optimization_barrier((column, own))
        other = lax.ppermute(own, "c", [(0, 1), (1, 0)])
        column, back = lax.optimization_barrier((column, back))
        shares = lax.all_to_all(column.reshape(n_zh, deep, 2 * rank), "zh", 0, 0, tiled=True)
        down_share, up_t_share = pl.pallas_call(
            last_sum_kernel,
            out_shape=(jax.ShapeDtypeStruct((2 * quarter, rank), f32), jax.ShapeDtypeStruct((few, rank), f32)),
            grid=(1,),
            in_specs=[one(n_zh, deep, 2 * rank)],
            out_specs=(one(2 * quarter, rank), one(few, rank)),
            compiler_params=params(),
        )(shares)
        up_share = up_t_share.T

    with jax.named_scope("input_grad"):
        halves = 1
        several = n_y // halves
        wide = several * 2 * part
        order = (n_y, n_zh, part, kv_width)

        def block(*shape):
            return pl.BlockSpec(shape, lambda i, place: (0,) * len(shape))


        def weight_at(i, place):
            return i % halves, lax.rem(place[2] - i // halves + n_zh, n_zh), 0, 0

        weight_spec = pl.BlockSpec((several, 1, part, kv_width), weight_at)
        rows_spec = pl.BlockSpec((per_device, wide), lambda i, place: (0, i))
        input_grad = pl.pallas_call(
            final_kernel,
            out_shape=jax.ShapeDtypeStruct((per_device, features), bf16),
            grid_spec=pltpu.PrefetchScalarGridSpec(
                num_scalar_prefetch=1,
                grid=(features // wide,),
                in_specs=[
                    scalars(),
                    block(1, per_device),
                    block(per_device, kv_width),
                    weight_spec,
                    weight_spec,
                    rows_spec,
                ],
                out_specs=rows_spec,
                scratch_shapes=[pltpu.VMEM((per_device, per_device), bf16)],
            ),
            compiler_params=params(WHOLE_VMEM),
        )(
            place,
            live_row_counts,
            row_packing_order,
            output_gradient_rows,
            own.reshape(order),
            other.reshape(order),
            back,
        )
    return (input_grad, down_share[None], up_share[None])


def solution(mesh, parts=(4, 8, 2, 3, 4)):
    fine = Mesh(np.asarray(mesh.devices).reshape(parts), FSDP + DP)
    rows = P(FSDP + DP, None)
    in_specs = (
        rows,
        rows,
        P(FSDP, None),
        P(DP, None, None),
        P(DP, None, None),
        rows,
        rows,
    )
    out_specs = (rows, P(DP, FSDP, None), P(DP, None, FSDP))
    return jax.shard_map(on_device, mesh=fine, in_specs=in_specs, out_specs=out_specs, check_vma=False)
```

```python
import functools

import jax
import jax.numpy as jnp
import numpy as np
from jax import lax
from jax.experimental import pallas as pl
from jax.experimental.pallas import tpu as pltpu
from jax.sharding import Mesh, PartitionSpec as P

ADAPTER_SCALING = 2.0
FSDP = ("zh", "yh", "yl", "c")
DP = ("zl", "x")
VMEM_LIMIT = 16 * 1024 * 1024
WHOLE_VMEM = 60 * 1024 * 1024
NT = (((1,), (1,)), ((), ()))
NN = (((1,), (0,)), ((), ()))
TN = (((0,), (0,)), ((), ()))


def dot(a, b, dims):
    return lax.dot_general(a, b, dims, preferred_element_type=jnp.float32)


def live_one_hot(counts_ref, packing_ref):
    per_device = packing_ref.shape[1]
    tasks = counts_ref.shape[1]
    slot = per_device // tasks
    lane = lax.broadcasted_iota(jnp.int32, (1, per_device), 1)
    key = jnp.full((1, per_device), -1, jnp.int32)
    packing = packing_ref[...]
    for t in range(tasks):
        mine = (lane >= t * slot) & (lane < t * slot + counts_ref[0, t])
        key = jnp.where(mine, packing, key)
    row = lax.broadcasted_iota(jnp.int32, (per_device, per_device), 0)
    return jnp.where(row == key, 1.0, 0.0).astype(jnp.bfloat16)


def pack_kernel(counts_hbm, packing_hbm, rows_hbm, grads_hbm, out_hbm, counts, packing, held, packed, few_sems, in_sems, out_sems):
    features = rows_hbm.shape[1]
    width = grads_hbm.shape[1]
    pieces = in_sems.shape[0]
    step = features // (pieces - 1)
    spans = [pl.ds(at * step, step) for at in range(pieces - 1)] + [pl.ds(features, width)]
    small = (
        pltpu.make_async_copy(counts_hbm, counts, few_sems.at[0]),
        pltpu.make_async_copy(packing_hbm, packing, few_sems.at[1]),
    )
    loads = []
    for at, span in enumerate(spans):
        source = grads_hbm if at == pieces - 1 else rows_hbm.at[:, span]
        loads.append(pltpu.make_async_copy(source, held.at[:, span], in_sems.at[at]))
    for copy in (*small, *loads):
        copy.start()
    for copy in small:
        copy.wait()
    chosen = live_one_hot(counts, packing)
    stores = []
    for at, span in enumerate(spans):
        loads[at].wait()
        packed[:, span] = dot(chosen, held[:, span], TN).astype(jnp.bfloat16)
        stores.append(pltpu.make_async_copy(packed.at[:, span], out_hbm.at[:, span], out_sems.at[at]))
        stores[at].start()
    for copy in stores:
        copy.wait()


def adapter_kernel(place_ref, recv_ref, down_t_ref, up_ref, dx_ref, keep_ref, send_ref):
    rank, features = down_t_ref.shape
    blocks = 2 * keep_ref.shape[1]
    first = place_ref[0] == 0
    wide = features // blocks
    half = wide // 2
    quarter = half // 2
    grads = recv_ref[:, features:]
    proj = dot(grads, up_ref[...], NT).astype(jnp.bfloat16)
    total = jnp.zeros((recv_ref.shape[0], rank), jnp.float32)
    step = 1024
    turn = [lax.bitwise_xor(place_ref[1], yl) for yl in range(2)]
    for at in range(0, features, step):
        rows = recv_ref[:, at : at + step]
        part = down_t_ref[:, at : at + step]
        dx_ref[:, at : at + step] = (ADAPTER_SCALING * dot(proj, part, NN)).astype(jnp.bfloat16)
        total = total + dot(rows, part, NT)
        down = ADAPTER_SCALING * dot(rows, proj, TN)
        for b in range(step // wide):
            pair_at, yl = divmod(at // wide + b, 2)
            pair = []
            for c in range(2):
                lo = b * wide + c * half
                pair.append(jnp.concatenate([down[lo : lo + quarter], down[lo + quarter : lo + half]], axis=1))
            keep_ref[turn[yl], pair_at, :quarter, :] = jnp.where(first, pair[0], pair[1])
            send_ref[turn[yl], pair_at, :quarter, :] = jnp.where(first, pair[1], pair[0])
    up_t = ADAPTER_SCALING * dot(grads, total.astype(jnp.bfloat16), TN)
    up_t = jnp.concatenate([up_t, jnp.zeros_like(up_t)], axis=1)
    few = grads.shape[1] // (2 * blocks)
    for b in range(blocks):
        pair_at, yl = divmod(b, 2)
        low, high = up_t[2 * b * few : (2 * b + 1) * few], up_t[(2 * b + 1) * few : (2 * b + 2) * few]
        keep_ref[turn[yl], pair_at, quarter:, :] = jnp.where(first, low, high)
        send_ref[turn[yl], pair_at, quarter:, :] = jnp.where(first, high, low)


def half_kernel(held_ref, got_ref, keep_ref, send_ref):
    keep_ref[...] = held_ref[0] + got_ref[0]
    send_ref[...] = (held_ref[1] + got_ref[1]).astype(send_ref.dtype)


def add_kernel(held_ref, got_ref, out_ref):
    out_ref[...] = (held_ref[...] + got_ref[...].astype(jnp.float32)).astype(out_ref.dtype)


def last_sum_kernel(got_ref, down_ref, up_t_ref):
    half, rank = down_ref.shape
    quarter = half // 2
    total = jnp.sum(got_ref[...].astype(jnp.float32), axis=0)
    down_ref[:quarter, :] = total[:quarter, :rank]
    down_ref[quarter:, :] = total[:quarter, rank:]
    up_t_ref[...] = total[quarter:, :rank]


def final_kernel(counts_ref, packing_ref, grads_ref, weight_ref, back_ref, out_ref, chosen_ref):
    @pl.when(pl.program_id(0) == 0)
    def _():
        chosen_ref[...] = live_one_hot(counts_ref, packing_ref)

    frozen = dot(grads_ref[...], weight_ref[...], NT).astype(jnp.bfloat16)
    placed = dot(chosen_ref[...], back_ref[...], NN)
    out_ref[...] = (frozen.astype(jnp.float32) + placed).astype(jnp.bfloat16)


def one(*shape):
    return pl.BlockSpec(shape, lambda i: (0,) * len(shape))


def hbm():
    return pl.BlockSpec(memory_space=pltpu.HBM)


def scalars():
    return pl.BlockSpec(memory_space=pltpu.SMEM)


def params(limit=VMEM_LIMIT):
    return pltpu.CompilerParams(vmem_limit_bytes=limit)


def on_device(
    inputs,
    output_gradient_rows,
    fixed_value_weight,
    task_down_adapters,
    task_up_adapters,
    live_row_counts,
    row_packing_order,
):
    per_device, features = inputs.shape
    kv_width = output_gradient_rows.shape[1]
    tasks = lax.axis_size("zl") * lax.axis_size("x")
    slot = per_device // tasks
    n_zh, n_yh = lax.axis_size("zh"), lax.axis_size("yh")
    pairs = n_zh * n_yh
    blocks = 2 * pairs
    down_t = task_down_adapters[0].T
    up = task_up_adapters[0]
    rank = up.shape[0]
    bf16, f32 = jnp.bfloat16, jnp.float32
    place = jnp.stack([lax.axis_index("c"), lax.axis_index("yl")]).astype(jnp.int32)

    with jax.named_scope("frozen_gather"):
        weight = lax.all_gather(fixed_value_weight, FSDP, axis=0, tiled=True)

    with jax.named_scope("pack"):
        packed = pl.pallas_call(
            pack_kernel,
            out_shape=jax.ShapeDtypeStruct((per_device, features + kv_width), bf16),
            in_specs=[hbm(), hbm(), hbm(), hbm()],
            out_specs=hbm(),
            scratch_shapes=[
                pltpu.SMEM((1, tasks), jnp.int32),
                pltpu.VMEM((1, per_device), jnp.int32),
                pltpu.VMEM((per_device, features + kv_width), bf16),
                pltpu.VMEM((per_device, features + kv_width), bf16),
                pltpu.SemaphoreType.DMA((2,)),
                pltpu.SemaphoreType.DMA((5,)),
                pltpu.SemaphoreType.DMA((5,)),
            ],
            compiler_params=params(WHOLE_VMEM),
        )(live_row_counts, row_packing_order, inputs, output_gradient_rows)
        recv = lax.all_to_all(packed.reshape(tasks, slot, features + kv_width), DP, 0, 0, tiled=True)
        recv = recv.reshape(per_device, features + kv_width)

    with jax.named_scope("adapters"):
        quarter = features // (4 * blocks)
        few = kv_width // (2 * blocks)
        deep = quarter + few
        terms = jax.ShapeDtypeStruct((2, pairs, deep, 2 * rank), f32)
        dx, keep, send = pl.pallas_call(
            adapter_kernel,
            out_shape=(jax.ShapeDtypeStruct((per_device, features), bf16), terms, terms),
            grid=(1,),
            in_specs=[scalars(), one(per_device, features + kv_width), one(rank, features), one(rank, kv_width)],
            out_specs=(one(per_device, features), one(*terms.shape), one(*terms.shape)),
            compiler_params=params(),
        )(place, recv, down_t, up)
        back = lax.all_to_all(dx.reshape(tasks, slot, features), DP, 0, 0, tiled=True)
        back = back.reshape(per_device, features)

    with jax.named_scope("weight_grads"):
        flat = (pairs * deep, 2 * rank)
        held, got = keep.reshape(2, *flat), lax.ppermute(send.reshape(2, *flat), "c", [(0, 1), (1, 0)])
        held, away = pl.pallas_call(
            half_kernel,
            out_shape=(jax.ShapeDtypeStruct(flat, f32), jax.ShapeDtypeStruct(flat, bf16)),
            grid=(1,),
            in_specs=[one(2, *flat), one(2, *flat)],
            out_specs=(one(*flat), one(*flat)),
            compiler_params=params(),
        )(held, got)
        column = pl.pallas_call(
            add_kernel,
            out_shape=jax.ShapeDtypeStruct(flat, bf16),
            grid=(1,),
            in_specs=[one(*flat), one(*flat)],
            out_specs=one(*flat),
            compiler_params=params(),
        )(held, lax.ppermute(away, "yl", [(0, 1), (1, 0)]))
        column, back = lax.optimization_barrier((column, back))
        shares = lax.all_to_all(column.reshape(pairs, deep, 2 * rank), ("zh", "yh"), 0, 0, tiled=True)
        down_share, up_t_share = pl.pallas_call(
            last_sum_kernel,
            out_shape=(jax.ShapeDtypeStruct((2 * quarter, rank), f32), jax.ShapeDtypeStruct((few, rank), f32)),
            grid=(1,),
            in_specs=[one(pairs, deep, 2 * rank)],
            out_specs=(one(2 * quarter, rank), one(few, rank)),
            compiler_params=params(),
        )(shares)
        up_share = up_t_share.T

    with jax.named_scope("input_grad"):
        wide = features // 4
        rows_spec = pl.BlockSpec((per_device, wide), lambda i: (0, i))
        input_grad = pl.pallas_call(
            final_kernel,
            out_shape=jax.ShapeDtypeStruct((per_device, features), bf16),
            grid=(features // wide,),
            in_specs=[
                scalars(),
                one(1, per_device),
                one(per_device, kv_width),
                pl.BlockSpec((wide, kv_width), lambda i: (i, 0)),
                rows_spec,
            ],
            out_specs=rows_spec,
            scratch_shapes=[pltpu.VMEM((per_device, per_device), bf16)],
            compiler_params=params(WHOLE_VMEM),
        )(live_row_counts, row_packing_order, output_gradient_rows, weight, back)
    return (input_grad, down_share[None], up_share[None])


def solution(mesh, parts=(4, 4, 2, 2, 3, 4)):
    fine = Mesh(np.asarray(mesh.devices).reshape(parts), FSDP + DP)
    rows = P(FSDP + DP, None)
    in_specs = (
        rows,
        rows,
        P(FSDP, None),
        P(DP, None, None),
        P(DP, None, None),
        rows,
        rows,
    )
    out_specs = (rows, P(DP, FSDP, None), P(DP, None, FSDP))
    return jax.shard_map(on_device, mesh=fine, in_specs=in_specs, out_specs=out_specs, check_vma=False)
```

```python
import functools

import jax
import jax.numpy as jnp
import numpy as np
from jax import lax
from jax.experimental import pallas as pl
from jax.experimental.pallas import tpu as pltpu
from jax.sharding import Mesh, PartitionSpec as P

ADAPTER_SCALING = 2.0
FSDP = ("zh", "yh", "yl", "c")
DP = ("zl", "x")
VMEM_LIMIT = 16 * 1024 * 1024
WHOLE_VMEM = 60 * 1024 * 1024
NT = (((1,), (1,)), ((), ()))
NN = (((1,), (0,)), ((), ()))
TN = (((0,), (0,)), ((), ()))


def dot(a, b, dims):
    return lax.dot_general(a, b, dims, preferred_element_type=jnp.float32)


def live_one_hot(counts_ref, packing_ref):
    per_device = packing_ref.shape[1]
    tasks = counts_ref.shape[1]
    slot = per_device // tasks
    lane = lax.broadcasted_iota(jnp.int32, (1, per_device), 1)
    key = jnp.full((1, per_device), -1, jnp.int32)
    packing = packing_ref[...]
    for t in range(tasks):
        mine = (lane >= t * slot) & (lane < t * slot + counts_ref[0, t])
        key = jnp.where(mine, packing, key)
    row = lax.broadcasted_iota(jnp.int32, (per_device, per_device), 0)
    return jnp.where(row == key, 1.0, 0.0).astype(jnp.bfloat16)


def pack_kernel(counts_hbm, packing_hbm, rows_hbm, grads_hbm, out_hbm, counts, packing, held, packed, few_sems, in_sems, out_sems):
    features = rows_hbm.shape[1]
    width = grads_hbm.shape[1]
    pieces = in_sems.shape[0]
    step = features // (pieces - 1)
    spans = [pl.ds(at * step, step) for at in range(pieces - 1)] + [pl.ds(features, width)]
    small = (
        pltpu.make_async_copy(counts_hbm, counts, few_sems.at[0]),
        pltpu.make_async_copy(packing_hbm, packing, few_sems.at[1]),
    )
    loads = []
    for at, span in enumerate(spans):
        source = grads_hbm if at == pieces - 1 else rows_hbm.at[:, span]
        loads.append(pltpu.make_async_copy(source, held.at[:, span], in_sems.at[at]))
    for copy in (*small, *loads):
        copy.start()
    for copy in small:
        copy.wait()
    chosen = live_one_hot(counts, packing)
    stores = []
    for at, span in enumerate(spans):
        loads[at].wait()
        packed[:, span] = dot(chosen, held[:, span], TN).astype(jnp.bfloat16)
        stores.append(pltpu.make_async_copy(packed.at[:, span], out_hbm.at[:, span], out_sems.at[at]))
        stores[at].start()
    for copy in stores:
        copy.wait()


def adapter_kernel(place_ref, recv_ref, down_t_ref, up_ref, dx_ref, keep_ref, send_ref):
    rank, features = down_t_ref.shape
    blocks = 2 * keep_ref.shape[1]
    first = place_ref[0] == 0
    wide = features // blocks
    half = wide // 2
    quarter = half // 2
    grads = recv_ref[:, features:]
    proj = dot(grads, up_ref[...], NT).astype(jnp.bfloat16)
    total = jnp.zeros((recv_ref.shape[0], rank), jnp.float32)
    step = 1024
    turn = [lax.bitwise_xor(place_ref[1], yl) for yl in range(2)]
    for at in range(0, features, step):
        rows = recv_ref[:, at : at + step]
        part = down_t_ref[:, at : at + step]
        dx_ref[:, at : at + step] = (ADAPTER_SCALING * dot(proj, part, NN)).astype(jnp.bfloat16)
        total = total + dot(rows, part, NT)
        down = ADAPTER_SCALING * dot(rows, proj, TN)
        for b in range(step // wide):
            pair_at, yl = divmod(at // wide + b, 2)
            pair = []
            for c in range(2):
                lo = b * wide + c * half
                pair.append(jnp.concatenate([down[lo : lo + quarter], down[lo + quarter : lo + half]], axis=1))
            keep_ref[turn[yl], pair_at, :quarter, :] = jnp.where(first, pair[0], pair[1])
            send_ref[turn[yl], pair_at, :quarter, :] = jnp.where(first, pair[1], pair[0])
    up_t = ADAPTER_SCALING * dot(grads, total.astype(jnp.bfloat16), TN)
    up_t = jnp.concatenate([up_t, jnp.zeros_like(up_t)], axis=1)
    few = grads.shape[1] // (2 * blocks)
    for b in range(blocks):
        pair_at, yl = divmod(b, 2)
        low, high = up_t[2 * b * few : (2 * b + 1) * few], up_t[(2 * b + 1) * few : (2 * b + 2) * few]
        keep_ref[turn[yl], pair_at, quarter:, :] = jnp.where(first, low, high)
        send_ref[turn[yl], pair_at, quarter:, :] = jnp.where(first, high, low)


def half_kernel(held_ref, got_ref, keep_ref, send_ref):
    keep_ref[...] = held_ref[0] + got_ref[0]
    send_ref[...] = (held_ref[1] + got_ref[1]).astype(send_ref.dtype)


def add_kernel(held_ref, got_ref, out_ref):
    out_ref[...] = (held_ref[...] + got_ref[...].astype(jnp.float32)).astype(out_ref.dtype)


def last_sum_kernel(got_ref, down_ref, up_t_ref):
    half, rank = down_ref.shape
    quarter = half // 2
    total = jnp.sum(got_ref[...].astype(jnp.float32), axis=0)
    down_ref[:quarter, :] = total[:quarter, :rank]
    down_ref[quarter:, :] = total[:quarter, rank:]
    up_t_ref[...] = total[quarter:, :rank]


def final_kernel(place_ref, counts_ref, packing_ref, grads_ref, own_ref, other_ref, back_ref, out_ref, chosen_ref):
    @pl.when(pl.program_id(0) == 0)
    def _():
        chosen_ref[...] = live_one_hot(counts_ref, packing_ref)

    first = place_ref[0] == 0
    several, _, part, depth = own_ref.shape
    own, other = own_ref[:, 0], other_ref[:, 0]
    low = jnp.where(first, own, other)
    high = jnp.where(first, other, own)
    weight = jnp.concatenate([low, high], axis=1).reshape(several * 2 * part, depth)
    frozen = dot(grads_ref[...], weight, NT).astype(jnp.bfloat16)
    placed = dot(chosen_ref[...], back_ref[...], NN)
    out_ref[...] = (frozen.astype(jnp.float32) + placed).astype(jnp.bfloat16)


def one(*shape):
    return pl.BlockSpec(shape, lambda i: (0,) * len(shape))


def hbm():
    return pl.BlockSpec(memory_space=pltpu.HBM)


def scalars():
    return pl.BlockSpec(memory_space=pltpu.SMEM)


def params(limit=VMEM_LIMIT):
    return pltpu.CompilerParams(vmem_limit_bytes=limit)


def on_device(
    inputs,
    output_gradient_rows,
    fixed_value_weight,
    task_down_adapters,
    task_up_adapters,
    live_row_counts,
    row_packing_order,
):
    per_device, features = inputs.shape
    kv_width = output_gradient_rows.shape[1]
    tasks = lax.axis_size("zl") * lax.axis_size("x")
    slot = per_device // tasks
    n_zh, n_yh = lax.axis_size("zh"), lax.axis_size("yh")
    pairs = n_zh * n_yh
    blocks = 2 * pairs
    part = fixed_value_weight.shape[0]
    down_t = task_down_adapters[0].T
    up = task_up_adapters[0]
    rank = up.shape[0]
    bf16, f32 = jnp.bfloat16, jnp.float32
    place = jnp.stack([lax.axis_index("c"), lax.axis_index("yl")]).astype(jnp.int32)

    with jax.named_scope("frozen_gather"):
        spread = jnp.broadcast_to(fixed_value_weight[None], (n_zh, part, kv_width))
        along_z = lax.all_to_all(spread, "zh", 0, 0, tiled=True).reshape(n_zh * part, kv_width)

    with jax.named_scope("pack"):
        packed = pl.pallas_call(
            pack_kernel,
            out_shape=jax.ShapeDtypeStruct((per_device, features + kv_width), bf16),
            in_specs=[hbm(), hbm(), hbm(), hbm()],
            out_specs=hbm(),
            scratch_shapes=[
                pltpu.SMEM((1, tasks), jnp.int32),
                pltpu.VMEM((1, per_device), jnp.int32),
                pltpu.VMEM((per_device, features + kv_width), bf16),
                pltpu.VMEM((per_device, features + kv_width), bf16),
                pltpu.SemaphoreType.DMA((2,)),
                pltpu.SemaphoreType.DMA((5,)),
                pltpu.SemaphoreType.DMA((5,)),
            ],
            compiler_params=params(WHOLE_VMEM),
        )(live_row_counts, row_packing_order, inputs, output_gradient_rows)
        packed, along_z = lax.optimization_barrier((packed, along_z))
        own = lax.all_gather(along_z, ("yh", "yl"), axis=0, tiled=True)
        recv = lax.all_to_all(packed.reshape(tasks, slot, features + kv_width), DP, 0, 0, tiled=True)
        recv = recv.reshape(per_device, features + kv_width)

    with jax.named_scope("adapters"):
        quarter = features // (4 * blocks)
        few = kv_width // (2 * blocks)
        deep = quarter + few
        terms = jax.ShapeDtypeStruct((2, pairs, deep, 2 * rank), f32)
        dx, keep, send = pl.pallas_call(
            adapter_kernel,
            out_shape=(jax.ShapeDtypeStruct((per_device, features), bf16), terms, terms),
            grid=(1,),
            in_specs=[scalars(), one(per_device, features + kv_width), one(rank, features), one(rank, kv_width)],
            out_specs=(one(per_device, features), one(*terms.shape), one(*terms.shape)),
            compiler_params=params(),
        )(place, recv, down_t, up)
        back = lax.all_to_all(dx.reshape(tasks, slot, features), DP, 0, 0, tiled=True)
        back = back.reshape(per_device, features)

    with jax.named_scope("weight_grads"):
        flat = (pairs * deep, 2 * rank)
        held, got = keep.reshape(2, *flat), lax.ppermute(send.reshape(2, *flat), "c", [(0, 1), (1, 0)])
        held, away = pl.pallas_call(
            half_kernel,
            out_shape=(jax.ShapeDtypeStruct(flat, f32), jax.ShapeDtypeStruct(flat, bf16)),
            grid=(1,),
            in_specs=[one(2, *flat), one(2, *flat)],
            out_specs=(one(*flat), one(*flat)),
            compiler_params=params(),
        )(held, got)
        column = pl.pallas_call(
            add_kernel,
            out_shape=jax.ShapeDtypeStruct(flat, bf16),
            grid=(1,),
            in_specs=[one(*flat), one(*flat)],
            out_specs=one(*flat),
            compiler_params=params(),
        )(held, lax.ppermute(away, "yl", [(0, 1), (1, 0)]))
        column, own = lax.optimization_barrier((column, own))
        other = lax.ppermute(own, "c", [(0, 1), (1, 0)])
        column, back = lax.optimization_barrier((column, back))
        shares = lax.all_to_all(column.reshape(pairs, deep, 2 * rank), ("zh", "yh"), 0, 0, tiled=True)
        down_share, up_t_share = pl.pallas_call(
            last_sum_kernel,
            out_shape=(jax.ShapeDtypeStruct((2 * quarter, rank), f32), jax.ShapeDtypeStruct((few, rank), f32)),
            grid=(1,),
            in_specs=[one(pairs, deep, 2 * rank)],
            out_specs=(one(2 * quarter, rank), one(few, rank)),
            compiler_params=params(),
        )(shares)
        up_share = up_t_share.T

    with jax.named_scope("input_grad"):
        n_y = 2 * n_yh
        wide = n_y * 2 * part
        order = (n_y, n_zh, part, kv_width)

        def block(*shape):
            return pl.BlockSpec(shape, lambda i, place: (0,) * len(shape))

        weight_spec = pl.BlockSpec((n_y, 1, part, kv_width), lambda i, place: (0, i, 0, 0))
        rows_spec = pl.BlockSpec((per_device, wide), lambda i, place: (0, i))
        input_grad = pl.pallas_call(
            final_kernel,
            out_shape=jax.ShapeDtypeStruct((per_device, features), bf16),
            grid_spec=pltpu.PrefetchScalarGridSpec(
                num_scalar_prefetch=1,
                grid=(features // wide,),
                in_specs=[
                    scalars(),
                    block(1, per_device),
                    block(per_device, kv_width),
                    weight_spec,
                    weight_spec,
                    rows_spec,
                ],
                out_specs=rows_spec,
                scratch_shapes=[pltpu.VMEM((per_device, per_device), bf16)],
            ),
            compiler_params=params(WHOLE_VMEM),
        )(
            place,
            live_row_counts,
            row_packing_order,
            output_gradient_rows,
            own.reshape(order),
            other.reshape(order),
            back,
        )
    return (input_grad, down_share[None], up_share[None])


def solution(mesh, parts=(4, 4, 2, 2, 3, 4)):
    fine = Mesh(np.asarray(mesh.devices).reshape(parts), FSDP + DP)
    rows = P(FSDP + DP, None)
    in_specs = (
        rows,
        rows,
        P(FSDP, None),
        P(DP, None, None),
        P(DP, None, None),
        rows,
        rows,
    )
    out_specs = (rows, P(DP, FSDP, None), P(DP, None, FSDP))
    return jax.shard_map(on_device, mesh=fine, in_specs=in_specs, out_specs=out_specs, check_vma=False)
```

```python
import functools

import jax
import jax.numpy as jnp
import numpy as np
from jax import lax
from jax.experimental import pallas as pl
from jax.experimental.pallas import tpu as pltpu
from jax.sharding import Mesh, PartitionSpec as P

ADAPTER_SCALING = 2.0
FSDP = ("zh", "yh", "yl", "c")
DP = ("zl", "x")
VMEM_LIMIT = 16 * 1024 * 1024
WHOLE_VMEM = 60 * 1024 * 1024
NT = (((1,), (1,)), ((), ()))
NN = (((1,), (0,)), ((), ()))
TN = (((0,), (0,)), ((), ()))


def dot(a, b, dims):
    return lax.dot_general(a, b, dims, preferred_element_type=jnp.float32)


def live_one_hot(counts_ref, packing_ref):
    per_device = packing_ref.shape[1]
    tasks = counts_ref.shape[1]
    slot = per_device // tasks
    lane = lax.broadcasted_iota(jnp.int32, (1, per_device), 1)
    key = jnp.full((1, per_device), -1, jnp.int32)
    packing = packing_ref[...]
    for t in range(tasks):
        mine = (lane >= t * slot) & (lane < t * slot + counts_ref[0, t])
        key = jnp.where(mine, packing, key)
    row = lax.broadcasted_iota(jnp.int32, (per_device, per_device), 0)
    return jnp.where(row == key, 1.0, 0.0).astype(jnp.bfloat16)


def pack_kernel(counts_hbm, packing_hbm, rows_hbm, grads_hbm, out_hbm, counts, packing, held, packed, few_sems, in_sems, out_sems):
    features = rows_hbm.shape[1]
    width = grads_hbm.shape[1]
    pieces = in_sems.shape[0]
    step = features // (pieces - 1)
    spans = [pl.ds(at * step, step) for at in range(pieces - 1)] + [pl.ds(features, width)]
    small = (
        pltpu.make_async_copy(counts_hbm, counts, few_sems.at[0]),
        pltpu.make_async_copy(packing_hbm, packing, few_sems.at[1]),
    )
    loads = []
    for at, span in enumerate(spans):
        source = grads_hbm if at == pieces - 1 else rows_hbm.at[:, span]
        loads.append(pltpu.make_async_copy(source, held.at[:, span], in_sems.at[at]))
    for copy in (*small, *loads):
        copy.start()
    for copy in small:
        copy.wait()
    chosen = live_one_hot(counts, packing)
    stores = []
    for at, span in enumerate(spans):
        loads[at].wait()
        packed[:, span] = dot(chosen, held[:, span], TN).astype(jnp.bfloat16)
        stores.append(pltpu.make_async_copy(packed.at[:, span], out_hbm.at[:, span], out_sems.at[at]))
        stores[at].start()
    for copy in stores:
        copy.wait()


def input_grad_kernel(grads_ref, down_t_ref, up_ref, dx_ref):
    proj = dot(grads_ref[...], up_ref[...], NT).astype(jnp.bfloat16)
    features = down_t_ref.shape[1]
    step = 1024
    for at in range(0, features, step):
        dx = ADAPTER_SCALING * dot(proj, down_t_ref[:, at : at + step], NN)
        dx_ref[:, at : at + step] = dx.astype(jnp.bfloat16)


def weight_grad_kernel(place_ref, recv_ref, down_t_ref, up_ref, keep_ref, send_ref):
    rank, features = down_t_ref.shape
    blocks = 2 * keep_ref.shape[1]
    first = place_ref[0] == 0
    wide = features // blocks
    half = wide // 2
    quarter = half // 2
    grads = recv_ref[:, features:]
    proj = dot(grads, up_ref[...], NT).astype(jnp.bfloat16)
    total = jnp.zeros((recv_ref.shape[0], rank), jnp.float32)
    step = 1024
    turn = [lax.bitwise_xor(place_ref[1], yl) for yl in range(2)]
    for at in range(0, features, step):
        rows = recv_ref[:, at : at + step]
        part = down_t_ref[:, at : at + step]
        total = total + dot(rows, part, NT)
        down = ADAPTER_SCALING * dot(rows, proj, TN)
        for b in range(step // wide):
            pair_at, yl = divmod(at // wide + b, 2)
            pair = []
            for c in range(2):
                lo = b * wide + c * half
                pair.append(jnp.concatenate([down[lo : lo + quarter], down[lo + quarter : lo + half]], axis=1))
            keep_ref[turn[yl], pair_at, :quarter, :] = jnp.where(first, pair[0], pair[1])
            send_ref[turn[yl], pair_at, :quarter, :] = jnp.where(first, pair[1], pair[0])
    up_t = ADAPTER_SCALING * dot(grads, total.astype(jnp.bfloat16), TN)
    up_t = jnp.concatenate([up_t, jnp.zeros_like(up_t)], axis=1)
    few = grads.shape[1] // (2 * blocks)
    for b in range(blocks):
        pair_at, yl = divmod(b, 2)
        low, high = up_t[2 * b * few : (2 * b + 1) * few], up_t[(2 * b + 1) * few : (2 * b + 2) * few]
        keep_ref[turn[yl], pair_at, quarter:, :] = jnp.where(first, low, high)
        send_ref[turn[yl], pair_at, quarter:, :] = jnp.where(first, high, low)


def half_kernel(held_ref, got_ref, keep_ref, send_ref):
    keep_ref[...] = held_ref[0] + got_ref[0]
    send_ref[...] = (held_ref[1] + got_ref[1]).astype(send_ref.dtype)


def add_kernel(held_ref, got_ref, out_ref):
    out_ref[...] = (held_ref[...] + got_ref[...].astype(jnp.float32)).astype(out_ref.dtype)


def last_sum_kernel(got_ref, down_ref, up_t_ref):
    half, rank = down_ref.shape
    quarter = half // 2
    total = jnp.sum(got_ref[...].astype(jnp.float32), axis=0)
    down_ref[:quarter, :] = total[:quarter, :rank]
    down_ref[quarter:, :] = total[:quarter, rank:]
    up_t_ref[...] = total[quarter:, :rank]


def final_kernel(place_ref, counts_ref, packing_ref, grads_ref, own_ref, other_ref, back_ref, out_ref, chosen_ref):
    @pl.when(pl.program_id(0) == 0)
    def _():
        chosen_ref[...] = live_one_hot(counts_ref, packing_ref)

    first = place_ref[0] == 0
    several, _, part, depth = own_ref.shape
    own, other = own_ref[:, 0], other_ref[:, 0]
    low = jnp.where(first, own, other)
    high = jnp.where(first, other, own)
    weight = jnp.concatenate([low, high], axis=1).reshape(several * 2 * part, depth)
    frozen = dot(grads_ref[...], weight, NT).astype(jnp.bfloat16)
    placed = dot(chosen_ref[...], back_ref[...], NN)
    out_ref[...] = (frozen.astype(jnp.float32) + placed).astype(jnp.bfloat16)


def one(*shape):
    return pl.BlockSpec(shape, lambda i: (0,) * len(shape))


def hbm():
    return pl.BlockSpec(memory_space=pltpu.HBM)


def scalars():
    return pl.BlockSpec(memory_space=pltpu.SMEM)


def params(limit=VMEM_LIMIT):
    return pltpu.CompilerParams(vmem_limit_bytes=limit)


def on_device(
    inputs,
    output_gradient_rows,
    fixed_value_weight,
    task_down_adapters,
    task_up_adapters,
    live_row_counts,
    row_packing_order,
):
    per_device, features = inputs.shape
    kv_width = output_gradient_rows.shape[1]
    tasks = lax.axis_size("zl") * lax.axis_size("x")
    slot = per_device // tasks
    n_zh, n_yh = lax.axis_size("zh"), lax.axis_size("yh")
    pairs = n_zh * n_yh
    blocks = 2 * pairs
    part = fixed_value_weight.shape[0]
    down_t = task_down_adapters[0].T
    up = task_up_adapters[0]
    rank = up.shape[0]
    bf16, f32 = jnp.bfloat16, jnp.float32
    place = jnp.stack([lax.axis_index("c"), lax.axis_index("yl"), lax.axis_index("zh")]).astype(jnp.int32)

    with jax.named_scope("frozen_gather"):
        along_z = [fixed_value_weight]
        for shift in range(1, n_zh):
            along_z.append(lax.ppermute(fixed_value_weight, "zh", [(i, (i + shift) % n_zh) for i in range(n_zh)]))

    with jax.named_scope("pack"):
        packed = pl.pallas_call(
            pack_kernel,
            out_shape=jax.ShapeDtypeStruct((per_device, features + kv_width), bf16),
            in_specs=[hbm(), hbm(), hbm(), hbm()],
            out_specs=hbm(),
            scratch_shapes=[
                pltpu.SMEM((1, tasks), jnp.int32),
                pltpu.VMEM((1, per_device), jnp.int32),
                pltpu.VMEM((per_device, features + kv_width), bf16),
                pltpu.VMEM((per_device, features + kv_width), bf16),
                pltpu.SemaphoreType.DMA((2,)),
                pltpu.SemaphoreType.DMA((5,)),
                pltpu.SemaphoreType.DMA((5,)),
            ],
            compiler_params=params(WHOLE_VMEM),
        )(live_row_counts, row_packing_order, inputs, output_gradient_rows)
        packed, *along_z = lax.optimization_barrier((packed, *along_z))
        own = lax.all_gather(jnp.concatenate(along_z, axis=0), ("yh", "yl"), axis=0, tiled=True)
        recv = lax.all_to_all(packed.reshape(tasks, slot, features + kv_width), DP, 0, 0, tiled=True)
        recv = recv.reshape(per_device, features + kv_width)

    with jax.named_scope("adapters"):
        quarter = features // (4 * blocks)
        few = kv_width // (2 * blocks)
        deep = quarter + few
        terms = jax.ShapeDtypeStruct((2, pairs, deep, 2 * rank), f32)
        dx = pl.pallas_call(
            input_grad_kernel,
            out_shape=jax.ShapeDtypeStruct((per_device, features), bf16),
            grid=(1,),
            in_specs=[
                pl.BlockSpec((per_device, kv_width), lambda i: (0, features // kv_width)),
                one(rank, features),
                one(rank, kv_width),
            ],
            out_specs=one(per_device, features),
            compiler_params=params(),
        )(recv, down_t, up)
        keep, send = pl.pallas_call(
            weight_grad_kernel,
            out_shape=(terms, terms),
            grid=(1,),
            in_specs=[scalars(), one(per_device, features + kv_width), one(rank, features), one(rank, kv_width)],
            out_specs=(one(*terms.shape), one(*terms.shape)),
            compiler_params=params(),
        )(place, recv, down_t, up)
        back = lax.all_to_all(dx.reshape(tasks, slot, features), DP, 0, 0, tiled=True)
        back = back.reshape(per_device, features)

    with jax.named_scope("weight_grads"):
        flat = (pairs * deep, 2 * rank)
        held, got = keep.reshape(2, *flat), lax.ppermute(send.reshape(2, *flat), "c", [(0, 1), (1, 0)])
        held, away = pl.pallas_call(
            half_kernel,
            out_shape=(jax.ShapeDtypeStruct(flat, f32), jax.ShapeDtypeStruct(flat, bf16)),
            grid=(1,),
            in_specs=[one(2, *flat), one(2, *flat)],
            out_specs=(one(*flat), one(*flat)),
            compiler_params=params(),
        )(held, got)
        column = pl.pallas_call(
            add_kernel,
            out_shape=jax.ShapeDtypeStruct(flat, bf16),
            grid=(1,),
            in_specs=[one(*flat), one(*flat)],
            out_specs=one(*flat),
            compiler_params=params(),
        )(held, lax.ppermute(away, "yl", [(0, 1), (1, 0)]))
        column, own = lax.optimization_barrier((column, own))
        other = lax.ppermute(own, "c", [(0, 1), (1, 0)])
        column, back = lax.optimization_barrier((column, back))
        shares = lax.all_to_all(column.reshape(pairs, deep, 2 * rank), ("zh", "yh"), 0, 0, tiled=True)
        down_share, up_t_share = pl.pallas_call(
            last_sum_kernel,
            out_shape=(jax.ShapeDtypeStruct((2 * quarter, rank), f32), jax.ShapeDtypeStruct((few, rank), f32)),
            grid=(1,),
            in_specs=[one(pairs, deep, 2 * rank)],
            out_specs=(one(2 * quarter, rank), one(few, rank)),
            compiler_params=params(),
        )(shares)
        up_share = up_t_share.T

    with jax.named_scope("input_grad"):
        n_y = 2 * n_yh
        wide = n_y * 2 * part
        order = (n_y, n_zh, part, kv_width)

        def block(*shape):
            return pl.BlockSpec(shape, lambda i, place: (0,) * len(shape))

        def weight_at(i, place):
            return 0, lax.rem(place[2] - i + n_zh, n_zh), 0, 0

        weight_spec = pl.BlockSpec((n_y, 1, part, kv_width), weight_at)
        rows_spec = pl.BlockSpec((per_device, wide), lambda i, place: (0, i))
        input_grad = pl.pallas_call(
            final_kernel,
            out_shape=jax.ShapeDtypeStruct((per_device, features), bf16),
            grid_spec=pltpu.PrefetchScalarGridSpec(
                num_scalar_prefetch=1,
                grid=(features // wide,),
                in_specs=[
                    scalars(),
                    block(1, per_device),
                    block(per_device, kv_width),
                    weight_spec,
                    weight_spec,
                    rows_spec,
                ],
                out_specs=rows_spec,
                scratch_shapes=[pltpu.VMEM((per_device, per_device), bf16)],
            ),
            compiler_params=params(WHOLE_VMEM),
        )(
            place,
            live_row_counts,
            row_packing_order,
            output_gradient_rows,
            own.reshape(order),
            other.reshape(order),
            back,
        )
    return (input_grad, down_share[None], up_share[None])


def solution(mesh, parts=(4, 4, 2, 2, 3, 4)):
    fine = Mesh(np.asarray(mesh.devices).reshape(parts), FSDP + DP)
    rows = P(FSDP + DP, None)
    in_specs = (
        rows,
        rows,
        P(FSDP, None),
        P(DP, None, None),
        P(DP, None, None),
        rows,
        rows,
    )
    out_specs = (rows, P(DP, FSDP, None), P(DP, None, FSDP))
    return jax.shard_map(on_device, mesh=fine, in_specs=in_specs, out_specs=out_specs, check_vma=False)
```

```python
import functools

import jax
import jax.numpy as jnp
import numpy as np
from jax import lax
from jax.experimental import pallas as pl
from jax.experimental.pallas import tpu as pltpu
from jax.sharding import Mesh, PartitionSpec as P

ADAPTER_SCALING = 2.0
FSDP = ("zh", "yh", "yl", "c")
DP = ("zl", "x")
VMEM_LIMIT = 16 * 1024 * 1024
WHOLE_VMEM = 60 * 1024 * 1024
NT = (((1,), (1,)), ((), ()))
NN = (((1,), (0,)), ((), ()))
TN = (((0,), (0,)), ((), ()))


def dot(a, b, dims):
    return lax.dot_general(a, b, dims, preferred_element_type=jnp.float32)


def live_one_hot(counts_ref, packing_ref):
    per_device = packing_ref.shape[1]
    tasks = counts_ref.shape[1]
    slot = per_device // tasks
    lane = lax.broadcasted_iota(jnp.int32, (1, per_device), 1)
    key = jnp.full((1, per_device), -1, jnp.int32)
    packing = packing_ref[...]
    for t in range(tasks):
        mine = (lane >= t * slot) & (lane < t * slot + counts_ref[0, t])
        key = jnp.where(mine, packing, key)
    row = lax.broadcasted_iota(jnp.int32, (per_device, per_device), 0)
    return jnp.where(row == key, 1.0, 0.0).astype(jnp.bfloat16)


def pack_kernel(counts_hbm, packing_hbm, rows_hbm, grads_hbm, out_hbm, counts, packing, held, packed, few_sems, in_sems, out_sems):
    features = rows_hbm.shape[1]
    width = grads_hbm.shape[1]
    pieces = in_sems.shape[0]
    step = features // (pieces - 1)
    spans = [pl.ds(at * step, step) for at in range(pieces - 1)] + [pl.ds(features, width)]
    small = (
        pltpu.make_async_copy(counts_hbm, counts, few_sems.at[0]),
        pltpu.make_async_copy(packing_hbm, packing, few_sems.at[1]),
    )
    loads = []
    for at, span in enumerate(spans):
        source = grads_hbm if at == pieces - 1 else rows_hbm.at[:, span]
        loads.append(pltpu.make_async_copy(source, held.at[:, span], in_sems.at[at]))
    for copy in (*small, *loads):
        copy.start()
    for copy in small:
        copy.wait()
    chosen = live_one_hot(counts, packing)
    stores = []
    for at, span in enumerate(spans):
        loads[at].wait()
        packed[:, span] = dot(chosen, held[:, span], TN).astype(jnp.bfloat16)
        stores.append(pltpu.make_async_copy(packed.at[:, span], out_hbm.at[:, span], out_sems.at[at]))
        stores[at].start()
    for copy in stores:
        copy.wait()


def input_grad_kernel(grads_ref, down_t_ref, up_ref, dx_ref):
    proj = dot(grads_ref[...], up_ref[...], NT).astype(jnp.bfloat16)
    features = down_t_ref.shape[1]
    step = 1024
    for at in range(0, features, step):
        dx = ADAPTER_SCALING * dot(proj, down_t_ref[:, at : at + step], NN)
        dx_ref[:, at : at + step] = dx.astype(jnp.bfloat16)


def weight_grad_kernel(place_ref, recv_ref, down_t_ref, up_ref, keep_ref, send_ref):
    rank, features = down_t_ref.shape
    blocks = 2 * keep_ref.shape[1]
    first = place_ref[0] == 0
    wide = features // blocks
    half = wide // 2
    quarter = half // 2
    grads = recv_ref[:, features:]
    proj = dot(grads, up_ref[...], NT).astype(jnp.bfloat16)
    total = jnp.zeros((recv_ref.shape[0], rank), jnp.float32)
    step = 1024
    turn = [lax.bitwise_xor(place_ref[1], yl) for yl in range(2)]
    for at in range(0, features, step):
        rows = recv_ref[:, at : at + step]
        part = down_t_ref[:, at : at + step]
        total = total + dot(rows, part, NT)
        down = ADAPTER_SCALING * dot(rows, proj, TN)
        for b in range(step // wide):
            pair_at, yl = divmod(at // wide + b, 2)
            pair = []
            for c in range(2):
                lo = b * wide + c * half
                pair.append(jnp.concatenate([down[lo : lo + quarter], down[lo + quarter : lo + half]], axis=1))
            keep_ref[turn[yl], pair_at, :quarter, :] = jnp.where(first, pair[0], pair[1])
            send_ref[turn[yl], pair_at, :quarter, :] = jnp.where(first, pair[1], pair[0])
    up_t = ADAPTER_SCALING * dot(grads, total.astype(jnp.bfloat16), TN)
    up_t = jnp.concatenate([up_t, jnp.zeros_like(up_t)], axis=1)
    few = grads.shape[1] // (2 * blocks)
    for b in range(blocks):
        pair_at, yl = divmod(b, 2)
        low, high = up_t[2 * b * few : (2 * b + 1) * few], up_t[(2 * b + 1) * few : (2 * b + 2) * few]
        keep_ref[turn[yl], pair_at, quarter:, :] = jnp.where(first, low, high)
        send_ref[turn[yl], pair_at, quarter:, :] = jnp.where(first, high, low)


def half_kernel(held_ref, got_ref, keep_ref, send_ref):
    keep_ref[...] = held_ref[0] + got_ref[0]
    send_ref[...] = (held_ref[1] + got_ref[1]).astype(send_ref.dtype)


def add_kernel(held_ref, got_ref, out_ref):
    out_ref[...] = (held_ref[...] + got_ref[...].astype(jnp.float32)).astype(out_ref.dtype)


def last_sum_kernel(got_ref, down_ref, up_t_ref):
    half, rank = down_ref.shape
    quarter = half // 2
    total = jnp.sum(got_ref[...].astype(jnp.float32), axis=0)
    down_ref[:quarter, :] = total[:quarter, :rank]
    down_ref[quarter:, :] = total[:quarter, rank:]
    up_t_ref[...] = total[quarter:, :rank]


def final_kernel(place_ref, counts_ref, packing_ref, grads_ref, own_ref, other_ref, back_ref, out_ref, chosen_ref):
    @pl.when(pl.program_id(0) == 0)
    def _():
        chosen_ref[...] = live_one_hot(counts_ref, packing_ref)

    first = place_ref[0] == 0
    several, _, part, depth = own_ref.shape
    own, other = own_ref[:, 0], other_ref[:, 0]
    low = jnp.where(first, own, other)
    high = jnp.where(first, other, own)
    weight = jnp.concatenate([low, high], axis=1).reshape(several * 2 * part, depth)
    frozen = dot(grads_ref[...], weight, NT).astype(jnp.bfloat16)
    placed = dot(chosen_ref[...], back_ref[...], NN)
    out_ref[...] = (frozen.astype(jnp.float32) + placed).astype(jnp.bfloat16)


def one(*shape):
    return pl.BlockSpec(shape, lambda i: (0,) * len(shape))


def hbm():
    return pl.BlockSpec(memory_space=pltpu.HBM)


def scalars():
    return pl.BlockSpec(memory_space=pltpu.SMEM)


def params(limit=VMEM_LIMIT):
    return pltpu.CompilerParams(vmem_limit_bytes=limit)


def on_device(
    inputs,
    output_gradient_rows,
    fixed_value_weight,
    task_down_adapters,
    task_up_adapters,
    live_row_counts,
    row_packing_order,
):
    per_device, features = inputs.shape
    kv_width = output_gradient_rows.shape[1]
    tasks = lax.axis_size("zl") * lax.axis_size("x")
    slot = per_device // tasks
    n_zh, n_yh = lax.axis_size("zh"), lax.axis_size("yh")
    pairs = n_zh * n_yh
    blocks = 2 * pairs
    part = fixed_value_weight.shape[0]
    down_t = task_down_adapters[0].T
    up = task_up_adapters[0]
    rank = up.shape[0]
    bf16, f32 = jnp.bfloat16, jnp.float32
    place = jnp.stack([lax.axis_index("c"), lax.axis_index("yl"), lax.axis_index("zh")]).astype(jnp.int32)

    with jax.named_scope("frozen_gather"):
        along_z = fixed_value_weight
        for apart in (1, 3)[: n_zh // 2]:
            got = lax.ppermute(along_z, "zh", [(i, i ^ apart) for i in range(n_zh)])
            along_z = jnp.concatenate([along_z, got], axis=0)

    with jax.named_scope("pack"):
        packed = pl.pallas_call(
            pack_kernel,
            out_shape=jax.ShapeDtypeStruct((per_device, features + kv_width), bf16),
            in_specs=[hbm(), hbm(), hbm(), hbm()],
            out_specs=hbm(),
            scratch_shapes=[
                pltpu.SMEM((1, tasks), jnp.int32),
                pltpu.VMEM((1, per_device), jnp.int32),
                pltpu.VMEM((per_device, features + kv_width), bf16),
                pltpu.VMEM((per_device, features + kv_width), bf16),
                pltpu.SemaphoreType.DMA((2,)),
                pltpu.SemaphoreType.DMA((5,)),
                pltpu.SemaphoreType.DMA((5,)),
            ],
            compiler_params=params(WHOLE_VMEM),
        )(live_row_counts, row_packing_order, inputs, output_gradient_rows)
        packed, got = lax.optimization_barrier((packed, got))
        own = lax.all_gather(along_z, ("yh", "yl"), axis=0, tiled=True)
        recv = lax.all_to_all(packed.reshape(tasks, slot, features + kv_width), DP, 0, 0, tiled=True)
        recv = recv.reshape(per_device, features + kv_width)

    with jax.named_scope("adapters"):
        quarter = features // (4 * blocks)
        few = kv_width // (2 * blocks)
        deep = quarter + few
        terms = jax.ShapeDtypeStruct((2, pairs, deep, 2 * rank), f32)
        dx = pl.pallas_call(
            input_grad_kernel,
            out_shape=jax.ShapeDtypeStruct((per_device, features), bf16),
            grid=(1,),
            in_specs=[
                pl.BlockSpec((per_device, kv_width), lambda i: (0, features // kv_width)),
                one(rank, features),
                one(rank, kv_width),
            ],
            out_specs=one(per_device, features),
            compiler_params=params(),
        )(recv, down_t, up)
        keep, send = pl.pallas_call(
            weight_grad_kernel,
            out_shape=(terms, terms),
            grid=(1,),
            in_specs=[scalars(), one(per_device, features + kv_width), one(rank, features), one(rank, kv_width)],
            out_specs=(one(*terms.shape), one(*terms.shape)),
            compiler_params=params(),
        )(place, recv, down_t, up)
        back = lax.all_to_all(dx.reshape(tasks, slot, features), DP, 0, 0, tiled=True)
        back = back.reshape(per_device, features)

    with jax.named_scope("weight_grads"):
        flat = (pairs * deep, 2 * rank)
        held, got = keep.reshape(2, *flat), lax.ppermute(send.reshape(2, *flat), "c", [(0, 1), (1, 0)])
        held, away = pl.pallas_call(
            half_kernel,
            out_shape=(jax.ShapeDtypeStruct(flat, f32), jax.ShapeDtypeStruct(flat, bf16)),
            grid=(1,),
            in_specs=[one(2, *flat), one(2, *flat)],
            out_specs=(one(*flat), one(*flat)),
            compiler_params=params(),
        )(held, got)
        column = pl.pallas_call(
            add_kernel,
            out_shape=jax.ShapeDtypeStruct(flat, bf16),
            grid=(1,),
            in_specs=[one(*flat), one(*flat)],
            out_specs=one(*flat),
            compiler_params=params(),
        )(held, lax.ppermute(away, "yl", [(0, 1), (1, 0)]))
        column, own = lax.optimization_barrier((column, own))
        other = lax.ppermute(own, "c", [(0, 1), (1, 0)])
        column, back = lax.optimization_barrier((column, back))
        shares = lax.all_to_all(column.reshape(pairs, deep, 2 * rank), ("zh", "yh"), 0, 0, tiled=True)
        down_share, up_t_share = pl.pallas_call(
            last_sum_kernel,
            out_shape=(jax.ShapeDtypeStruct((2 * quarter, rank), f32), jax.ShapeDtypeStruct((few, rank), f32)),
            grid=(1,),
            in_specs=[one(pairs, deep, 2 * rank)],
            out_specs=(one(2 * quarter, rank), one(few, rank)),
            compiler_params=params(),
        )(shares)
        up_share = up_t_share.T

    with jax.named_scope("input_grad"):
        n_y = 2 * n_yh
        wide = n_y * 2 * part
        order = (n_y, n_zh, part, kv_width)

        def block(*shape):
            return pl.BlockSpec(shape, lambda i, place: (0,) * len(shape))

        def weight_at(i, place):
            apart = lax.bitwise_xor(place[2], i)
            return 0, lax.bitwise_xor(apart, apart // 2), 0, 0

        weight_spec = pl.BlockSpec((n_y, 1, part, kv_width), weight_at)
        rows_spec = pl.BlockSpec((per_device, wide), lambda i, place: (0, i))
        input_grad = pl.pallas_call(
            final_kernel,
            out_shape=jax.ShapeDtypeStruct((per_device, features), bf16),
            grid_spec=pltpu.PrefetchScalarGridSpec(
                num_scalar_prefetch=1,
                grid=(features // wide,),
                in_specs=[
                    scalars(),
                    block(1, per_device),
                    block(per_device, kv_width),
                    weight_spec,
                    weight_spec,
                    rows_spec,
                ],
                out_specs=rows_spec,
                scratch_shapes=[pltpu.VMEM((per_device, per_device), bf16)],
            ),
            compiler_params=params(WHOLE_VMEM),
        )(
            place,
            live_row_counts,
            row_packing_order,
            output_gradient_rows,
            own.reshape(order),
            other.reshape(order),
            back,
        )
    return (input_grad, down_share[None], up_share[None])


def solution(mesh, parts=(4, 4, 2, 2, 3, 4)):
    fine = Mesh(np.asarray(mesh.devices).reshape(parts), FSDP + DP)
    rows = P(FSDP + DP, None)
    in_specs = (
        rows,
        rows,
        P(FSDP, None),
        P(DP, None, None),
        P(DP, None, None),
        rows,
        rows,
    )
    out_specs = (rows, P(DP, FSDP, None), P(DP, None, FSDP))
    return jax.shard_map(on_device, mesh=fine, in_specs=in_specs, out_specs=out_specs, check_vma=False)
```

```python
import functools

import jax
import jax.numpy as jnp
import numpy as np
from jax import lax
from jax.experimental import pallas as pl
from jax.experimental.pallas import tpu as pltpu
from jax.sharding import Mesh, PartitionSpec as P

ADAPTER_SCALING = 2.0
FSDP = ("zh", "ya", "yb", "yl", "c")
DP = ("zl", "x")
VMEM_LIMIT = 16 * 1024 * 1024
WHOLE_VMEM = 60 * 1024 * 1024
NT = (((1,), (1,)), ((), ()))
NN = (((1,), (0,)), ((), ()))
TN = (((0,), (0,)), ((), ()))


def dot(a, b, dims):
    return lax.dot_general(a, b, dims, preferred_element_type=jnp.float32)


def live_one_hot(counts_ref, packing_ref):
    per_device = packing_ref.shape[1]
    tasks = counts_ref.shape[1]
    slot = per_device // tasks
    lane = lax.broadcasted_iota(jnp.int32, (1, per_device), 1)
    key = jnp.full((1, per_device), -1, jnp.int32)
    packing = packing_ref[...]
    for t in range(tasks):
        mine = (lane >= t * slot) & (lane < t * slot + counts_ref[0, t])
        key = jnp.where(mine, packing, key)
    row = lax.broadcasted_iota(jnp.int32, (per_device, per_device), 0)
    return jnp.where(row == key, 1.0, 0.0).astype(jnp.bfloat16)


def pack_kernel(counts_hbm, packing_hbm, rows_hbm, grads_hbm, out_hbm, counts, packing, held, packed, few_sems, in_sems, out_sems):
    features = rows_hbm.shape[1]
    width = grads_hbm.shape[1]
    pieces = in_sems.shape[0]
    step = features // (pieces - 1)
    spans = [pl.ds(at * step, step) for at in range(pieces - 1)] + [pl.ds(features, width)]
    small = (
        pltpu.make_async_copy(counts_hbm, counts, few_sems.at[0]),
        pltpu.make_async_copy(packing_hbm, packing, few_sems.at[1]),
    )
    loads = []
    for at, span in enumerate(spans):
        source = grads_hbm if at == pieces - 1 else rows_hbm.at[:, span]
        loads.append(pltpu.make_async_copy(source, held.at[:, span], in_sems.at[at]))
    for copy in (*small, *loads):
        copy.start()
    for copy in small:
        copy.wait()
    chosen = live_one_hot(counts, packing)
    stores = []
    for at, span in enumerate(spans):
        loads[at].wait()
        packed[:, span] = dot(chosen, held[:, span], TN).astype(jnp.bfloat16)
        stores.append(pltpu.make_async_copy(packed.at[:, span], out_hbm.at[:, span], out_sems.at[at]))
        stores[at].start()
    for copy in stores:
        copy.wait()


def input_grad_kernel(grads_ref, down_t_ref, up_ref, dx_ref):
    proj = dot(grads_ref[...], up_ref[...], NT).astype(jnp.bfloat16)
    features = down_t_ref.shape[1]
    step = 1024
    for at in range(0, features, step):
        dx = ADAPTER_SCALING * dot(proj, down_t_ref[:, at : at + step], NN)
        dx_ref[:, at : at + step] = dx.astype(jnp.bfloat16)


def weight_grad_kernel(place_ref, recv_ref, down_t_ref, up_ref, keep_ref, send_ref):
    rank, features = down_t_ref.shape
    blocks = 4 * keep_ref.shape[1]
    first = place_ref[0] == 0
    wide = features // blocks
    half = wide // 2
    quarter = half // 2
    grads = recv_ref[:, features:]
    proj = dot(grads, up_ref[...], NT).astype(jnp.bfloat16)
    total = jnp.zeros((recv_ref.shape[0], rank), jnp.float32)
    step = 1024
    turn = [2 * lax.bitwise_xor(place_ref[1], y % 2) + lax.bitwise_xor(place_ref[3], y // 2) for y in range(4)]
    for at in range(0, features, step):
        rows = recv_ref[:, at : at + step]
        part = down_t_ref[:, at : at + step]
        total = total + dot(rows, part, NT)
        down = ADAPTER_SCALING * dot(rows, proj, TN)
        for b in range(step // wide):
            pair_at, y = divmod(at // wide + b, 4)
            pair = []
            for c in range(2):
                lo = b * wide + c * half
                pair.append(jnp.concatenate([down[lo : lo + quarter], down[lo + quarter : lo + half]], axis=1))
            keep_ref[turn[y], pair_at, :quarter, :] = jnp.where(first, pair[0], pair[1])
            send_ref[turn[y], pair_at, :quarter, :] = jnp.where(first, pair[1], pair[0])
    up_t = ADAPTER_SCALING * dot(grads, total.astype(jnp.bfloat16), TN)
    up_t = jnp.concatenate([up_t, jnp.zeros_like(up_t)], axis=1)
    few = grads.shape[1] // (2 * blocks)
    for b in range(blocks):
        pair_at, y = divmod(b, 4)
        low, high = up_t[2 * b * few : (2 * b + 1) * few], up_t[(2 * b + 1) * few : (2 * b + 2) * few]
        keep_ref[turn[y], pair_at, quarter:, :] = jnp.where(first, low, high)
        send_ref[turn[y], pair_at, quarter:, :] = jnp.where(first, high, low)


def half_kernel(held_ref, got_ref, keep_ref, send_ref):
    keep_ref[...] = held_ref[0] + got_ref[0].astype(jnp.float32)
    send_ref[...] = (held_ref[1] + got_ref[1].astype(jnp.float32)).astype(send_ref.dtype)


def add_kernel(held_ref, got_ref, out_ref):
    out_ref[...] = (held_ref[...] + got_ref[...].astype(jnp.float32)).astype(out_ref.dtype)


def last_sum_kernel(got_ref, down_ref, up_t_ref):
    half, rank = down_ref.shape
    quarter = half // 2
    total = jnp.sum(got_ref[...].astype(jnp.float32), axis=0)
    down_ref[:quarter, :] = total[:quarter, :rank]
    down_ref[quarter:, :] = total[:quarter, rank:]
    up_t_ref[...] = total[quarter:, :rank]


def final_kernel(place_ref, counts_ref, packing_ref, grads_ref, own_ref, other_ref, back_ref, out_ref, chosen_ref):
    @pl.when(pl.program_id(0) == 0)
    def _():
        chosen_ref[...] = live_one_hot(counts_ref, packing_ref)

    first = place_ref[0] == 0
    several, _, part, depth = own_ref.shape
    own, other = own_ref[:, 0], other_ref[:, 0]
    low = jnp.where(first, own, other)
    high = jnp.where(first, other, own)
    weight = jnp.concatenate([low, high], axis=1).reshape(several * 2 * part, depth)
    frozen = dot(grads_ref[...], weight, NT).astype(jnp.bfloat16)
    placed = dot(chosen_ref[...], back_ref[...], NN)
    out_ref[...] = (frozen.astype(jnp.float32) + placed).astype(jnp.bfloat16)


def one(*shape):
    return pl.BlockSpec(shape, lambda i: (0,) * len(shape))


def hbm():
    return pl.BlockSpec(memory_space=pltpu.HBM)


def scalars():
    return pl.BlockSpec(memory_space=pltpu.SMEM)


def params(limit=VMEM_LIMIT):
    return pltpu.CompilerParams(vmem_limit_bytes=limit)


def on_device(
    inputs,
    output_gradient_rows,
    fixed_value_weight,
    task_down_adapters,
    task_up_adapters,
    live_row_counts,
    row_packing_order,
):
    per_device, features = inputs.shape
    kv_width = output_gradient_rows.shape[1]
    tasks = lax.axis_size("zl") * lax.axis_size("x")
    slot = per_device // tasks
    n_zh, n_ya = lax.axis_size("zh"), lax.axis_size("ya")
    pairs = n_zh * n_ya
    blocks = 4 * pairs
    part = fixed_value_weight.shape[0]
    down_t = task_down_adapters[0].T
    up = task_up_adapters[0]
    rank = up.shape[0]
    bf16, f32 = jnp.bfloat16, jnp.float32
    place = jnp.stack([lax.axis_index("c"), lax.axis_index("yl"), lax.axis_index("zh"), lax.axis_index("yb")]).astype(jnp.int32)

    with jax.named_scope("frozen_gather"):
        along_z = fixed_value_weight
        for apart in (1, 3)[: n_zh // 2]:
            got = lax.ppermute(along_z, "zh", [(i, i ^ apart) for i in range(n_zh)])
            along_z = jnp.concatenate([along_z, got], axis=0)

    with jax.named_scope("pack"):
        packed = pl.pallas_call(
            pack_kernel,
            out_shape=jax.ShapeDtypeStruct((per_device, features + kv_width), bf16),
            in_specs=[hbm(), hbm(), hbm(), hbm()],
            out_specs=hbm(),
            scratch_shapes=[
                pltpu.SMEM((1, tasks), jnp.int32),
                pltpu.VMEM((1, per_device), jnp.int32),
                pltpu.VMEM((per_device, features + kv_width), bf16),
                pltpu.VMEM((per_device, features + kv_width), bf16),
                pltpu.SemaphoreType.DMA((2,)),
                pltpu.SemaphoreType.DMA((5,)),
                pltpu.SemaphoreType.DMA((5,)),
            ],
            compiler_params=params(WHOLE_VMEM),
        )(live_row_counts, row_packing_order, inputs, output_gradient_rows)
        packed, got = lax.optimization_barrier((packed, got))
        own = lax.all_gather(along_z, ("ya", "yb", "yl"), axis=0, tiled=True)
        recv = lax.all_to_all(packed.reshape(tasks, slot, features + kv_width), DP, 0, 0, tiled=True)
        recv = recv.reshape(per_device, features + kv_width)

    with jax.named_scope("adapters"):
        quarter = features // (4 * blocks)
        few = kv_width // (2 * blocks)
        deep = quarter + few
        terms = jax.ShapeDtypeStruct((4, pairs, deep, 2 * rank), f32)
        dx = pl.pallas_call(
            input_grad_kernel,
            out_shape=jax.ShapeDtypeStruct((per_device, features), bf16),
            grid=(1,),
            in_specs=[
                pl.BlockSpec((per_device, kv_width), lambda i: (0, features // kv_width)),
                one(rank, features),
                one(rank, kv_width),
            ],
            out_specs=one(per_device, features),
            compiler_params=params(),
        )(recv, down_t, up)
        keep, send = pl.pallas_call(
            weight_grad_kernel,
            out_shape=(terms, terms),
            grid=(1,),
            in_specs=[scalars(), one(per_device, features + kv_width), one(rank, features), one(rank, kv_width)],
            out_specs=(one(*terms.shape), one(*terms.shape)),
            compiler_params=params(),
        )(place, recv, down_t, up)
        back = lax.all_to_all(dx.reshape(tasks, slot, features), DP, 0, 0, tiled=True)
        back = back.reshape(per_device, features)

    with jax.named_scope("weight_grads"):
        flat = (2 * pairs * deep, 2 * rank)
        held, got = keep.reshape(2, *flat), lax.ppermute(send.reshape(2, *flat), "c", [(0, 1), (1, 0)])
        for axis in ("yl", "yb"):
            held, away = pl.pallas_call(
                half_kernel,
                out_shape=(jax.ShapeDtypeStruct(flat, f32), jax.ShapeDtypeStruct(flat, bf16)),
                grid=(1,),
                in_specs=[one(2, *flat), one(2, *flat)],
                out_specs=(one(*flat), one(*flat)),
                compiler_params=params(),
            )(held, got)
            got = lax.ppermute(away, axis, [(0, 1), (1, 0)])
            if axis == "yl":
                flat = (pairs * deep, 2 * rank)
                held, got = held.reshape(2, *flat), got.reshape(2, *flat)
        column = pl.pallas_call(
            add_kernel,
            out_shape=jax.ShapeDtypeStruct(flat, bf16),
            grid=(1,),
            in_specs=[one(*flat), one(*flat)],
            out_specs=one(*flat),
            compiler_params=params(),
        )(held, got)
        column, own = lax.optimization_barrier((column, own))
        other = lax.ppermute(own, "c", [(0, 1), (1, 0)])
        column, back = lax.optimization_barrier((column, back))
        shares = lax.all_to_all(column.reshape(pairs, deep, 2 * rank), ("zh", "ya"), 0, 0, tiled=True)
        down_share, up_t_share = pl.pallas_call(
            last_sum_kernel,
            out_shape=(jax.ShapeDtypeStruct((2 * quarter, rank), f32), jax.ShapeDtypeStruct((few, rank), f32)),
            grid=(1,),
            in_specs=[one(pairs, deep, 2 * rank)],
            out_specs=(one(2 * quarter, rank), one(few, rank)),
            compiler_params=params(),
        )(shares)
        up_share = up_t_share.T

    with jax.named_scope("input_grad"):
        n_y = 4 * n_ya
        wide = n_y * 2 * part
        order = (n_y, n_zh, part, kv_width)

        def block(*shape):
            return pl.BlockSpec(shape, lambda i, place: (0,) * len(shape))

        def weight_at(i, place):
            apart = lax.bitwise_xor(place[2], i)
            return 0, lax.bitwise_xor(apart, apart // 2), 0, 0

        weight_spec = pl.BlockSpec((n_y, 1, part, kv_width), weight_at)
        rows_spec = pl.BlockSpec((per_device, wide), lambda i, place: (0, i))
        input_grad = pl.pallas_call(
            final_kernel,
            out_shape=jax.ShapeDtypeStruct((per_device, features), bf16),
            grid_spec=pltpu.PrefetchScalarGridSpec(
                num_scalar_prefetch=1,
                grid=(features // wide,),
                in_specs=[
                    scalars(),
                    block(1, per_device),
                    block(per_device, kv_width),
                    weight_spec,
                    weight_spec,
                    rows_spec,
                ],
                out_specs=rows_spec,
                scratch_shapes=[pltpu.VMEM((per_device, per_device), bf16)],
            ),
            compiler_params=params(WHOLE_VMEM),
        )(
            place,
            live_row_counts,
            row_packing_order,
            output_gradient_rows,
            own.reshape(order),
            other.reshape(order),
            back,
        )
    return (input_grad, down_share[None], up_share[None])


def solution(mesh, parts=(4, 2, 2, 2, 2, 3, 4)):
    fine = Mesh(np.asarray(mesh.devices).reshape(parts), FSDP + DP)
    rows = P(FSDP + DP, None)
    in_specs = (
        rows,
        rows,
        P(FSDP, None),
        P(DP, None, None),
        P(DP, None, None),
        rows,
        rows,
    )
    out_specs = (rows, P(DP, FSDP, None), P(DP, None, FSDP))
    return jax.shard_map(on_device, mesh=fine, in_specs=in_specs, out_specs=out_specs, check_vma=False)
```
